256 devices in a mesh: ctx: 16 (over y_hi, z), head: 16 (over y_lo, x, core).
Axes of the slice: x: 4, y: 4 (y_hi: 2, y_lo: 2; y = y_hi * 2 + y_lo), z: 8, core: 2. Of those that a mesh axis runs over, the one named last changes fastest.
Arguments:
- queries: bfloat16 [256, 128, 576], P('ctx', 'head'), may hold values from -48 to 48
- cache: bfloat16 [32768, 576], P('ctx'), may hold values from -6 to 6
- new_latents: bfloat16 [256, 576], P('ctx'), may hold values from -6 to 6
- cache_lengths: int32 [16], P('ctx'), may hold values from 1 to 2048, 20480 in all
- new_offsets: int32 [256], replicated, may hold values from 0 to 255, each once
- value_up_weight: bfloat16 [128, 512, 128], P('head'), may hold values from -6 to 6
Outputs:
- attention_out: bfloat16 [256, 128, 128], P('ctx', 'head')
The draws below stay inside these ranges and needn't reach their ends.
Inputs may be any that keep to these rules, and one draw needn't show every extreme that they name: Block b holds cache_lengths[b] valid rows; the largest is exactly 2048. `new_offsets`: each of 0 to 255 appears once.
All inputs are finite; a program needn't handle non-finite values.
Results may differ from the reference program's by a relative error of at most 0.015.
Values may be sent and summed in bfloat16 or wider, within the bound.
No kernel may reach another device: no remote copies, remote signals or barrier semaphores. Data moves between devices by JAX's collectives and lax.ppermute only.
A program may use at most 64 MiB of HBM per device.

```python
import math
import jax
import jax.numpy as jnp
import numpy as np
from jax import lax

KVR = 512
HEADS = 128
VDIM = 128
CACHE_DEV = 2048
LAT = 576
CONTEXT = 32768
NEW = 256
BLOCKS = 16
N_CTX = 16


def latent_table(key):
    return jnp.clip(jax.random.normal(key, (CONTEXT, LAT), jnp.float32), -6.0, 6.0)


def draw_cache(key, part):
    table = latent_table(key)
    return table.astype(jnp.bfloat16)


def draw_queries(key, part):
    key = jax.random.fold_in(key, 9)
    values = jnp.clip(jax.random.normal(key, (NEW, HEADS, LAT), jnp.float32), -6.0, 6.0)
    return values.astype(jnp.bfloat16)


def steps_of(own_key, extent, shards, least, top_value):
    factor_of, own = 1.0, jax.random.fold_in(own_key, 6)
    for position, parts in shards:
        steps = jnp.exp(jax.random.uniform(jax.random.fold_in(own, position), (parts,), jnp.float32, least / len(shards), top_value / len(shards)))
        factor_of = factor_of * jnp.repeat(steps, extent[position] // parts).reshape([-1 if axis == position else 1 for axis in range(len(extent))])
    return factor_of


def length_profile(amount, total, limit, lean):
    portions = [(1 << 20) // math.isqrt(grade ** lean) + 1 for grade in range(2, amount + 1)]
    surplus, given = total - limit - (amount - 1), [1] * (amount - 1)
    while surplus > 0:
        movable = [i for i in range(amount - 1) if given[i] < limit]
        whole, remaining = sum([portions[i] for i in movable]), surplus
        for i in movable:
            addition = min(limit - given[i], max(1, remaining * portions[i] // whole), surplus)
            given[i] = given[i] + addition
            surplus = surplus - addition
    return np.array([limit] + given)


def ragged_sizes(key, number_of, total, limit, slope):
    if number_of == 2:
        one = jax.random.randint(key, (), max(1, total - limit), min(limit, total - 1) + 1)
        return jnp.stack([one, total - one])
    lengths = jnp.asarray(length_profile(number_of, total, limit, slope), jnp.int32)
    couples = (number_of - 1) // 2
    giver, receiver = lengths[1:1 + 2 * couples:2], lengths[2:2 + 2 * couples:2]
    slack = jnp.minimum(giver - 1, limit - receiver)
    moved = jax.random.randint(jax.random.fold_in(key, 1), (couples,), 0, 1 << 20) % (slack + 1)
    lengths = lengths.at[1:1 + 2 * couples:2].set(giver - moved).at[2:2 + 2 * couples:2].set(receiver + moved)
    return lengths[jax.random.permutation(jax.random.fold_in(key, 2), number_of)]


def normal_values(stream_key, extent, width, reach, cuts=(), kind=jnp.bfloat16):
    gain = steps_of(stream_key, extent, cuts, -0.22, 0.18) if cuts else 1.0
    drawn = jax.random.normal(stream_key, extent, jnp.float32) * width * gain
    return jnp.minimum(jnp.maximum(drawn, -reach), reach).astype(kind)


def setup_inputs(seed: int = 0) -> dict:
    seeds = jax.random.split(jax.random.key(seed), 7)
    return {
        "queries": draw_queries(jax.random.fold_in(seeds[6], 71), 0),
        "cache": draw_cache(jax.random.fold_in(seeds[6], 71), 0),
        "new_latents": normal_values(seeds[2], (NEW, LAT), 1.0, 6.0, ((0, 16),)),
        "cache_lengths": ragged_sizes(seeds[3], BLOCKS, CACHE_DEV * N_CTX * 5 // 8, CACHE_DEV, 2).astype(jnp.int32),
        "new_offsets": jax.random.permutation(seeds[4], NEW).astype(jnp.int32),
        "value_up_weight": normal_values(seeds[5], (HEADS, KVR, VDIM), 1.0, 6.0, ((0, 16),)),
    }


softmax_scale = 192.0 ** -0.5
masked_value = -1e30


def reference(queries, cache, new_latents, cache_lengths, new_offsets, value_up_weight):
    query_rows = queries.reshape(NEW * HEADS, LAT)

    def visit_block(running, block_id):
        numer, highest, totals = running
        key_block = lax.dynamic_slice_in_dim(cache, block_id * CACHE_DEV, CACHE_DEV, 0)
        scores = jnp.dot(query_rows, key_block.T, preferred_element_type=jnp.float32) * softmax_scale
        valid = jnp.arange(CACHE_DEV, dtype=jnp.int32) < cache_lengths[block_id]
        scores = jnp.where(valid[None, :], scores, masked_value)
        block_max = jnp.max(scores, axis=1)
        weights = jnp.exp(scores - block_max[:, None])
        block_total = jnp.sum(weights, axis=1)
        block_values = jnp.dot(weights.astype(jnp.bfloat16), key_block[:, :KVR], preferred_element_type=jnp.float32)
        new_high = jnp.maximum(highest, block_max)
        previous_rescale_factor = jnp.exp(highest - new_high)
        new_factor = jnp.exp(block_max - new_high)
        numer = numer * previous_rescale_factor[:, None] + block_values * new_factor[:, None]
        totals = totals * previous_rescale_factor + block_total * new_factor
        return (numer, new_high, totals), None

    initial = (jnp.zeros((NEW * HEADS, KVR), jnp.float32),
               jnp.full((NEW * HEADS,), masked_value, jnp.float32),
               jnp.zeros((NEW * HEADS,), jnp.float32))
    (cache_numer, cache_high, cache_total), unused = lax.scan(visit_block, initial, jnp.arange(N_CTX, dtype=jnp.int32))
    cache_numer = cache_numer.reshape(NEW, HEADS, KVR)
    cache_high = cache_high.reshape(NEW, HEADS)
    cache_total = cache_total.reshape(NEW, HEADS)

    new_scores = jnp.dot(query_rows, new_latents.T, preferred_element_type=jnp.float32) * softmax_scale
    new_scores = new_scores.reshape(NEW, HEADS, NEW)
    allowed = new_offsets[None, :] <= new_offsets[:, None]
    new_scores = jnp.where(allowed[:, None, :], new_scores, masked_value)
    new_max = jnp.max(new_scores, axis=2)
    new_exp = jnp.exp(new_scores - new_max[:, :, None])
    new_total = jnp.sum(new_exp, axis=2)
    new_weights = new_exp.astype(jnp.bfloat16)
    new_values = jnp.einsum("thn,nk->thk", new_weights.astype(jnp.float32), new_latents[:, :KVR].astype(jnp.float32))

    overall = jnp.maximum(cache_high, new_max)
    cache_factor = jnp.exp(cache_high - overall)
    new_factor = jnp.exp(new_max - overall)
    numer = cache_numer * cache_factor[:, :, None] + new_values * new_factor[:, :, None]
    denom = cache_total * cache_factor + new_total * new_factor
    latent_output = numer / denom[:, :, None]
    final_output = jnp.einsum("ujc,jcn->ujn", latent_output, value_up_weight.astype(jnp.float32), precision=lax.Precision.HIGHEST)
    return final_output.astype(jnp.bfloat16)
```

```python
import functools

import jax
import jax.numpy as jnp
from jax import lax
from jax.experimental import pallas as pl
from jax.experimental.pallas import tpu as pltpu
from jax.sharding import PartitionSpec as P

KVR = 512
VDIM = 128
EXTRA = 32
STAT = 16
NZ = 8
OFFSETS = [0, 7, 1, 6, 2, 5, 3, 4]
SHARED = 256

exp_scale = 192.0 ** (-0.5) * 1.4426950408889634
masked_value = -1e30
NT = (((1,), (1,)), ((), ()))
small_cost = pl.CostEstimate(flops=10**6, bytes_accessed=10**4, transcendentals=0)
VMEM = pl.BlockSpec(memory_space=pltpu.VMEM)
SMEM = pl.BlockSpec(memory_space=pltpu.SMEM)


def dot_nt(a, b):
    return lax.dot_general(a, b, NT, preferred_element_type=jnp.float32)


def dot_nn(a, b):
    return jnp.dot(a, b, preferred_element_type=jnp.float32)


def pack_stats(high, total):
    lane = lax.broadcasted_iota(jnp.int32, (high.shape[0], 128), 1)
    return jnp.where(lane == 0, high, total)


def key_bias(width, valid):
    position = lax.broadcasted_iota(jnp.int32, (1, width), 1)
    return jnp.where(position < valid, 0.0, masked_value)


def pack_kernel(
    len_ref, keys_ref, new_ref, query_ref, shared_ref, direct_ref, rows_ref, stage_ref, new_vmem, query_vmem, flat_ref, sems
):
    head = lax.axis_index("head")
    core, side = lax.rem(head, 2), lax.rem(head // 2, 2)
    lat, few = shared_ref.shape
    width = direct_ref.shape[1]
    half = 2 * few + width
    own_tokens, heads, _ = query_ref.shape
    part = pl.multiple_of(core * half + side * few, 128)
    rest = pl.multiple_of(core * half + 2 * few, 128)
    load_query = pltpu.make_async_copy(query_ref, query_vmem, sems.at[0])
    load_new = pltpu.make_async_copy(new_ref, new_vmem, sems.at[1])
    load_shared = pltpu.make_async_copy(
        keys_ref.at[:, pl.ds(part, few)], stage_ref.at[0:lat, 0:few], sems.at[2]
    )
    load_direct = pltpu.make_async_copy(
        keys_ref.at[:, pl.ds(rest, width)], stage_ref.at[0:lat, few : few + width], sems.at[3]
    )
    send_shared = pltpu.make_async_copy(stage_ref.at[0:lat, 0:few], shared_ref, sems.at[4])
    send_direct = pltpu.make_async_copy(stage_ref.at[:, few : few + width], direct_ref, sems.at[5])
    load_shared.start()
    load_query.start()
    load_new.start()
    load_direct.start()
    length = len_ref[0]
    high = length // 256
    r = lax.broadcasted_iota(jnp.int32, (16, 128), 0)
    c = lax.broadcasted_iota(jnp.int32, (16, 128), 1)
    note = jnp.where(
        (r == 0) & (c == 0), high, jnp.where((r == 0) & (c == 1), length - high * 256, 0)
    ).astype(jnp.float32)
    stage_ref[lat + 16 : lat + 32, few + 128 : few + 256] = note.astype(jnp.bfloat16)
    load_shared.wait()
    send_shared.start()
    load_query.wait()
    queries = query_vmem[...].astype(jnp.float32).reshape(own_tokens * heads, lat)
    lanes = [slice(p, min(lat, p + 128)) for p in range(0, lat, 128)]
    for p, lane in enumerate(lanes):
        flat_ref[p, :, 0 : lane.stop - lane.start] = queries[:, lane]
    for one in range(heads):
        for p, lane in enumerate(lanes):
            rows = flat_ref[p, pl.ds(one, own_tokens, stride=heads), :]
            rows_ref[one * own_tokens : (one + 1) * own_tokens, lane] = rows[
                :, 0 : lane.stop - lane.start
            ].astype(jnp.bfloat16)
    load_new.wait()
    stage_ref[lat : lat + 16, few : few + KVR] = new_vmem[:, 0:KVR]
    stage_ref[lat + 16 : lat + 32, few : few + lat - KVR] = new_vmem[:, KVR:lat]
    load_direct.wait()
    send_direct.start()
    send_shared.wait()
    send_direct.wait()


def join_kernel(mine_ref, other_ref, direct_ref, near_ref):
    side = lax.rem(lax.axis_index("head") // 2, 2)
    lat, few = mine_ref.shape
    near_ref[0:lat, pl.ds(pl.multiple_of(side * few, 128), few)] = mine_ref[...]
    near_ref[0:lat, pl.ds(pl.multiple_of((1 - side) * few, 128), few)] = other_ref[...]
    near_ref[:, 2 * few :] = direct_ref[...]
    near_ref[lat:, 0 : 2 * few] = jnp.zeros((EXTRA, 2 * few), jnp.bfloat16)


def own_kernel(blocks, len_ref, *refs):
    query_refs, (keys_ref, acc_ref, stat_ref) = refs[:blocks], refs[blocks:]
    valid = len_ref[0]
    full = keys_ref.shape[1]
    widths = [full // 2, full * 3 // 4, full]

    def attend(width):
        rows = jnp.concatenate([r[...] for r in query_refs], axis=0)
        scores = dot_nn(rows, keys_ref[:, 0:width]) + key_bias(width, valid)
        high = jnp.max(scores, axis=1, keepdims=True)
        weights = jnp.exp2((scores - high) * exp_scale)
        total = jnp.sum(weights, axis=1, keepdims=True)
        acc_ref[...] = dot_nt(weights.astype(jnp.bfloat16), keys_ref[0:KVR, 0:width])
        stat_ref[...] = pack_stats(high, total)

    least = 0
    for width in widths:
        pl.when((valid > least) & (valid <= width))(functools.partial(attend, width))
        least = width


def attend_own(valid, blocks, keys):
    rows = sum(b.shape[0] for b in blocks)
    width = keys.shape[1]
    return pl.pallas_call(
        functools.partial(own_kernel, len(blocks)),
        in_specs=[SMEM] + [VMEM] * (len(blocks) + 1),
        out_specs=[VMEM, VMEM],
        out_shape=[
            jax.ShapeDtypeStruct((rows, KVR), jnp.float32),
            jax.ShapeDtypeStruct((rows, 128), jnp.float32),
        ],
        compiler_params=pltpu.CompilerParams(vmem_limit_bytes=12 * 2**20),
        cost_estimate=small_cost,
        name="attend_own",
    )(valid, *blocks, keys)


def partner_length(part_ref):
    lat = part_ref.shape[0] - EXTRA
    row = part_ref[lat + 16 : lat + 32, 2 * SHARED + 128 : 2 * SHARED + 256].astype(jnp.float32)
    r = lax.broadcasted_iota(jnp.int32, row.shape, 0)
    c = lax.broadcasted_iota(jnp.int32, row.shape, 1)
    high = jnp.sum(jnp.where((r == 0) & (c == 0), row, 0.0))
    low = jnp.sum(jnp.where((r == 0) & (c == 1), row, 0.0))
    return (high * 256.0 + low).astype(jnp.int32)


def fold(scores, values, acc, high, total):
    new_high = functools.reduce(
        jnp.maximum, [jnp.max(s, axis=1, keepdims=True) for s in scores], high
    )
    rescale = jnp.exp2((high - new_high) * exp_scale)
    acc = acc * rescale
    total = total * rescale
    for s, v in zip(scores, values):
        weights = jnp.exp2((s - new_high) * exp_scale)
        total = total + jnp.sum(weights, axis=1, keepdims=True)
        acc = acc + v(weights.astype(jnp.bfloat16))
    return acc, new_high, total


def final_kernel(counts, offset_ref, *refs):
    queries, refs = refs[:NZ], refs[NZ:]
    states, refs = refs[: 2 * len(counts)], refs[2 * len(counts) :]
    near_ref, far_ref, new_ref, up_ref, out_ref, latent_ref = refs
    pieces = [(g, 128 * i) for g, count in enumerate(counts) for i in range(count)]
    lat, width = near_ref.shape[0] - EXTRA, near_ref.shape[1]
    core = lax.rem(lax.axis_index("head"), 2)
    ctx = lax.axis_index("ctx")
    z, pair = lax.rem(ctx, NZ), ctx // NZ
    length = partner_length(near_ref)
    near_bias = key_bias(width, length - core * width)
    far_bias = key_bias(width, length - (1 - core) * width)
    first = 2 * SHARED
    partner_new = jnp.concatenate(
        [near_ref[lat : lat + 16, first : first + KVR], near_ref[lat + 16 : lat + 32, first : first + lat - KVR]],
        axis=1,
    )
    new_keys = jnp.concatenate([new_ref[...], partner_new], axis=0)
    lane = lax.broadcasted_iota(jnp.int32, (16, 32), 1)
    line = lax.broadcasted_iota(jnp.int32, (16, 32), 0)
    key_offsets = jnp.zeros((16, 32), jnp.int32)
    for k in range(32):
        side = pair if k < 16 else 1 - pair
        key_offsets = jnp.where(lane == k, offset_ref[(side * NZ + z) * 16 + k % 16], key_offsets)
    new_bias = []
    for block in range(NZ):
        first = (pair * NZ + lax.rem(z + OFFSETS[block], NZ)) * 16
        token_offsets = jnp.zeros((16, 32), jnp.int32)
        for t in range(16):
            token_offsets = jnp.where(line == t, offset_ref[first + t], token_offsets)
        new_bias.append(jnp.where(key_offsets <= token_offsets, 0.0, masked_value))
    wide = lax.broadcasted_iota(jnp.int32, (128, 128), 1)
    levels = jnp.zeros((128, 128), jnp.float32)
    for tile in range(NZ // 2):
        both = pieces[2 * tile : 2 * tile + 2]
        rows = jnp.concatenate([queries[2 * tile][...], queries[2 * tile + 1][...]], axis=0)
        stat = jnp.concatenate([states[2 * g + 1][r : r + 128, :] for g, r in both], axis=0)
        acc, high, total = fold(
            [
                dot_nn(rows, near_ref[0:lat, :]) + near_bias,
                dot_nn(rows, far_ref[0:lat, :]) + far_bias,
                dot_nt(rows, new_keys)
                + jnp.concatenate([new_bias[2 * tile]] * 8 + [new_bias[2 * tile + 1]] * 8, axis=0),
            ],
            [
                lambda w: dot_nt(w, near_ref[0:KVR, :]),
                lambda w: dot_nt(w, far_ref[0:KVR, :]),
                lambda w: dot_nn(w, new_keys[:, 0:KVR]),
            ],
            jnp.concatenate([states[2 * g][r : r + 128, :] for g, r in both], axis=0),
            stat[:, 0:1],
            stat[:, 1:2],
        )
        latent_ref[tile * 256 : (tile + 1) * 256, :] = (acc * (1.0 / total)).astype(jnp.bfloat16)
        level = high * exp_scale + jnp.log2(total)
        levels = jnp.where(wide == 2 * tile, level[:128], levels)
        levels = jnp.where(wide == 2 * tile + 1, level[128:], levels)
    slots = [lax.rem(z + OFFSETS[block], NZ) for block in range(NZ)]
    for head in range(8):
        latent = jnp.concatenate(
            [latent_ref[b * 128 + head * 16 : b * 128 + head * 16 + 16, :] for b in range(NZ)], axis=0
        )
        result = dot_nn(latent, up_ref[head]).astype(jnp.bfloat16)
        for block in range(NZ):
            out_ref[slots[block], head * 16 : head * 16 + 16, :] = result[block * 16 : block * 16 + 16]
    flat = levels.T
    p0 = flat.astype(jnp.bfloat16).astype(jnp.float32)
    p1 = (flat - p0).astype(jnp.bfloat16).astype(jnp.float32)
    p2 = flat - p0 - p1
    r = lax.broadcasted_iota(jnp.int32, (STAT, 128), 0)
    for block in range(NZ):
        stats = jnp.where(
            r == 0,
            p0[block : block + 1],
            jnp.where(r == 1, p1[block : block + 1], jnp.where(r == 2, p2[block : block + 1], 0.0)),
        )
        out_ref[slots[block], 128 : 128 + STAT, :] = stats.astype(jnp.bfloat16)


def merge_kernel(part_ref, out_ref, order_ref):
    levels = []
    for source in range(NZ):
        stats = part_ref[source, 128 : 128 + STAT, :].astype(jnp.float32)
        levels.append(stats[0:1] + stats[1:2] + stats[2:3])
    level = jnp.concatenate(levels, axis=0)
    factor = jnp.exp2(level - jnp.max(level, axis=0, keepdims=True))
    factor = factor / jnp.sum(factor, axis=0, keepdims=True)
    factor = jnp.concatenate([factor, jnp.zeros((128 - NZ, 128), jnp.float32)], axis=0).T
    total = jnp.zeros((128, VDIM), jnp.float32)
    for source in range(NZ):
        total = total + part_ref[source, 0:128, :].astype(jnp.float32) * factor[:, source : source + 1]
    for head in range(8):
        order_ref[pl.ds(head, 16, stride=8), :] = total[head * 16 : head * 16 + 16]
    out_ref[...] = order_ref[...].astype(jnp.bfloat16)


def shards(queries, cache, new_latents, cache_lengths, new_offsets, value_up_weight):
    own_tokens, head_local, lat = queries.shape
    rows = own_tokens * head_local
    z = lax.axis_index("ctx") % NZ
    keys = cache.T

    def across(a):
        moves = [
            (c * 16 + h, ((c + NZ) % 16) * 16 + (h + 8) % 16) for c in range(16) for h in range(16)
        ]
        return lax.ppermute(a, ("ctx", "head"), moves)

    def swap(a):
        return lax.ppermute(a, "head", [(h, h ^ 1) for h in range(16)])

    def shift(a, step):
        return lax.ppermute(
            a, "ctx", [(c, c // NZ * NZ + (c + step) % NZ) for c in range(16)]
        )

    width = cache.shape[0] // 2
    hbm = pl.BlockSpec(memory_space=pltpu.HBM)
    shared, direct, own = pl.pallas_call(
        pack_kernel,
        in_specs=[SMEM, hbm, hbm, hbm],
        out_specs=[hbm, hbm, VMEM],
        out_shape=[
            jax.ShapeDtypeStruct((lat, SHARED), jnp.bfloat16),
            jax.ShapeDtypeStruct((lat + EXTRA, width - 2 * SHARED), jnp.bfloat16),
            jax.ShapeDtypeStruct((rows, lat), jnp.bfloat16),
        ],
        scratch_shapes=[
            pltpu.VMEM((lat + EXTRA, width - SHARED), jnp.bfloat16),
            pltpu.VMEM((own_tokens, lat), jnp.bfloat16),
            pltpu.VMEM((own_tokens, head_local, lat), jnp.bfloat16),
            pltpu.VMEM((-(-lat // 128), rows, 128), jnp.float32),
            pltpu.SemaphoreType.DMA((6,)),
        ],
        compiler_params=pltpu.CompilerParams(vmem_limit_bytes=4 * 2**20),
        name="pack",
    )(
        cache_lengths,
        pltpu.with_memory_space_constraint(keys, pltpu.HBM),
        pltpu.with_memory_space_constraint(new_latents, pltpu.HBM),
        pltpu.with_memory_space_constraint(queries, pltpu.HBM),
    )
    mine = across(shared)

    state0 = attend_own(cache_lengths, [own], keys)
    up1, down1 = shift(own, 1), shift(own, -1)
    up1, down1, state0, direct = lax.optimization_barrier((up1, down1, state0, direct))
    direct = across(direct)
    up2, down2 = shift(up1, 1), shift(down1, -1)
    state1 = attend_own(cache_lengths, [up1, down1], keys)
    up2, down2, state1, mine = lax.optimization_barrier((up2, down2, state1, mine))
    other = lax.ppermute(mine, "head", [(h, h ^ 2) for h in range(16)])
    up3, down3 = shift(up2, 1), shift(down2, -1)
    four = lax.ppermute(
        jnp.where(z % 2 == 0, up2, down2),
        "ctx",
        [(c, c // NZ * NZ + (c + (2 if c % 2 == 0 else -2)) % NZ) for c in range(16)],
    )
    state2 = attend_own(cache_lengths, [up2, down2], keys)
    up3, down3, four, state2, other, direct = lax.optimization_barrier(
        (up3, down3, four, state2, other, direct)
    )
    near = pl.pallas_call(
        join_kernel,
        in_specs=[VMEM] * 3,
        out_specs=VMEM,
        out_shape=jax.ShapeDtypeStruct((lat + EXTRA, width), jnp.bfloat16),
        compiler_params=pltpu.CompilerParams(vmem_limit_bytes=6 * 2**20),
        cost_estimate=small_cost,
        name="join",
    )(mine, other, direct)
    far = swap(near)
    state3 = attend_own(cache_lengths, [up3, down3, four], keys)
    far, state3 = lax.optimization_barrier((far, state3))
    states = [part for state in (state0, state1, state2, state3) for part in state]
    parts = pl.pallas_call(
        functools.partial(final_kernel, [1, 2, 2, 3]),
        in_specs=[SMEM] + [VMEM] * (NZ + 12),
        out_specs=VMEM,
        out_shape=jax.ShapeDtypeStruct((NZ, rows + STAT, VDIM), jnp.bfloat16),
        scratch_shapes=[pltpu.VMEM((NZ * rows, KVR), jnp.bfloat16)],
        compiler_params=pltpu.CompilerParams(vmem_limit_bytes=16 * 2**20),
        cost_estimate=small_cost,
        name="attend_final",
    )(new_offsets, own, up1, down1, up2, down2, up3, down3, four, *states, near, far, new_latents, value_up_weight)
    got = lax.all_to_all(
        parts, "ctx", 0, 0, axis_index_groups=[[*range(NZ)], [*range(NZ, 2 * NZ)]], tiled=True
    )
    out = pl.pallas_call(
        merge_kernel,
        in_specs=[VMEM],
        out_specs=VMEM,
        out_shape=jax.ShapeDtypeStruct((rows, VDIM), jnp.bfloat16),
        scratch_shapes=[pltpu.VMEM((rows, VDIM), jnp.float32)],
        name="merge",
    )(got)
    return out.reshape(own_tokens, head_local, VDIM)


def solution(mesh):
    return jax.shard_map(
        shards,
        mesh=mesh,
        in_specs=(
            P("ctx", "head", None),
            P("ctx", None),
            P("ctx", None),
            P("ctx"),
            P(),
            P("head", None, None),
        ),
        out_specs=P("ctx", "head", None),
        check_vma=False,
    )
```

```python
import functools

import jax
import jax.numpy as jnp
from jax import lax
from jax.experimental import pallas as pl
from jax.experimental.pallas import tpu as pltpu
from jax.sharding import PartitionSpec as P

KVR = 512
VDIM = 128
EXTRA = 32
STAT = 16
NZ = 8
OFFSETS = [0, 7, 1, 6, 2, 5, 3, 4]
SHARED = 256

exp_scale = 192.0 ** (-0.5) * 1.4426950408889634
masked_value = -1e30
NT = (((1,), (1,)), ((), ()))
small_cost = pl.CostEstimate(flops=10**6, bytes_accessed=10**4, transcendentals=0)
VMEM = pl.BlockSpec(memory_space=pltpu.VMEM)
SMEM = pl.BlockSpec(memory_space=pltpu.SMEM)


def dot_nt(a, b):
    return lax.dot_general(a, b, NT, preferred_element_type=jnp.float32)


def dot_nn(a, b):
    return jnp.dot(a, b, preferred_element_type=jnp.float32)


def pack_stats(high, total):
    lane = lax.broadcasted_iota(jnp.int32, (high.shape[0], 128), 1)
    return jnp.where(lane == 0, high, total)


def key_bias(width, valid):
    position = lax.broadcasted_iota(jnp.int32, (1, width), 1)
    return jnp.where(position < valid, 0.0, masked_value)


def pack_kernel(
    len_ref, keys_ref, new_ref, query_ref, shared_ref, direct_ref, rows_ref, stage_ref, new_vmem, query_vmem, flat_ref, sems
):
    head = lax.axis_index("head")
    core, side = lax.rem(head, 2), lax.rem(head // 2, 2)
    lat, few = shared_ref.shape
    width = direct_ref.shape[1]
    half = 2 * few + width
    own_tokens, heads, _ = query_ref.shape
    part = pl.multiple_of(core * half + side * few, 128)
    rest = pl.multiple_of(core * half + 2 * few, 128)
    load_query = pltpu.make_async_copy(query_ref, query_vmem, sems.at[0])
    load_new = pltpu.make_async_copy(new_ref, new_vmem, sems.at[1])
    load_shared = pltpu.make_async_copy(
        keys_ref.at[:, pl.ds(part, few)], stage_ref.at[0:lat, 0:few], sems.at[2]
    )
    load_direct = pltpu.make_async_copy(
        keys_ref.at[:, pl.ds(rest, width)], stage_ref.at[0:lat, few : few + width], sems.at[3]
    )
    send_shared = pltpu.make_async_copy(stage_ref.at[0:lat, 0:few], shared_ref, sems.at[4])
    send_direct = pltpu.make_async_copy(stage_ref.at[:, few : few + width], direct_ref, sems.at[5])
    load_shared.start()
    load_query.start()
    load_new.start()
    load_direct.start()
    length = len_ref[0]
    high = length // 256
    r = lax.broadcasted_iota(jnp.int32, (16, 128), 0)
    c = lax.broadcasted_iota(jnp.int32, (16, 128), 1)
    note = jnp.where(
        (r == 0) & (c == 0), high, jnp.where((r == 0) & (c == 1), length - high * 256, 0)
    ).astype(jnp.float32)
    stage_ref[lat + 16 : lat + 32, few + 128 : few + 256] = note.astype(jnp.bfloat16)
    load_shared.wait()
    send_shared.start()
    load_query.wait()
    queries = query_vmem[...].astype(jnp.float32).reshape(own_tokens * heads, lat)
    lanes = [slice(p, min(lat, p + 128)) for p in range(0, lat, 128)]
    for p, lane in enumerate(lanes):
        flat_ref[p, :, 0 : lane.stop - lane.start] = queries[:, lane]
    for one in range(heads):
        for p, lane in enumerate(lanes):
            rows = flat_ref[p, pl.ds(one, own_tokens, stride=heads), :]
            rows_ref[one * own_tokens : (one + 1) * own_tokens, lane] = rows[
                :, 0 : lane.stop - lane.start
            ].astype(jnp.bfloat16)
    load_new.wait()
    stage_ref[lat : lat + 16, few : few + KVR] = new_vmem[:, 0:KVR]
    stage_ref[lat + 16 : lat + 32, few : few + lat - KVR] = new_vmem[:, KVR:lat]
    load_direct.wait()
    send_direct.start()
    send_shared.wait()
    send_direct.wait()


def join_kernel(mine_ref, other_ref, direct_ref, near_ref):
    side = lax.rem(lax.axis_index("head") // 2, 2)
    lat, few = mine_ref.shape
    near_ref[0:lat, pl.ds(pl.multiple_of(side * few, 128), few)] = mine_ref[...]
    near_ref[0:lat, pl.ds(pl.multiple_of((1 - side) * few, 128), few)] = other_ref[...]
    near_ref[:, 2 * few :] = direct_ref[...]
    near_ref[lat:, 0 : 2 * few] = jnp.zeros((EXTRA, 2 * few), jnp.bfloat16)


def own_kernel(blocks, len_ref, *refs):
    query_refs, (keys_ref, acc_ref, stat_ref) = refs[:blocks], refs[blocks:]
    valid = len_ref[0]
    full = keys_ref.shape[1]
    widths = [full // 2, full * 3 // 4, full]

    def attend(width):
        rows = jnp.concatenate([r[...] for r in query_refs], axis=0)
        scores = dot_nn(rows, keys_ref[:, 0:width]) + key_bias(width, valid)
        high = jnp.max(scores, axis=1, keepdims=True)
        weights = jnp.exp2((scores - high) * exp_scale)
        total = jnp.sum(weights, axis=1, keepdims=True)
        acc_ref[...] = dot_nt(weights.astype(jnp.bfloat16), keys_ref[0:KVR, 0:width])
        stat_ref[...] = pack_stats(high, total)

    least = 0
    for width in widths:
        pl.when((valid > least) & (valid <= width))(functools.partial(attend, width))
        least = width


def attend_own(valid, blocks, keys):
    rows = sum(b.shape[0] for b in blocks)
    width = keys.shape[1]
    return pl.pallas_call(
        functools.partial(own_kernel, len(blocks)),
        in_specs=[SMEM] + [VMEM] * (len(blocks) + 1),
        out_specs=[VMEM, VMEM],
        out_shape=[
            jax.ShapeDtypeStruct((rows, KVR), jnp.float32),
            jax.ShapeDtypeStruct((rows, 128), jnp.float32),
        ],
        compiler_params=pltpu.CompilerParams(vmem_limit_bytes=12 * 2**20),
        cost_estimate=small_cost,
        name="attend_own",
    )(valid, *blocks, keys)


def partner_length(part_ref):
    lat = part_ref.shape[0] - EXTRA
    row = part_ref[lat + 16 : lat + 32, 2 * SHARED + 128 : 2 * SHARED + 256].astype(jnp.float32)
    r = lax.broadcasted_iota(jnp.int32, row.shape, 0)
    c = lax.broadcasted_iota(jnp.int32, row.shape, 1)
    high = jnp.sum(jnp.where((r == 0) & (c == 0), row, 0.0))
    low = jnp.sum(jnp.where((r == 0) & (c == 1), row, 0.0))
    return (high * 256.0 + low).astype(jnp.int32)


def fold(scores, values, acc, high, total):
    new_high = functools.reduce(
        jnp.maximum, [jnp.max(s, axis=1, keepdims=True) for s in scores], high
    )
    rescale = jnp.exp2((high - new_high) * exp_scale)
    acc = acc * rescale
    total = total * rescale
    for s, v in zip(scores, values):
        weights = jnp.exp2((s - new_high) * exp_scale)
        total = total + jnp.sum(weights, axis=1, keepdims=True)
        acc = acc + v(weights.astype(jnp.bfloat16))
    return acc, new_high, total


def final_kernel(counts, offset_ref, *refs):
    queries, refs = refs[:NZ], refs[NZ:]
    states, refs = refs[: 2 * len(counts)], refs[2 * len(counts) :]
    near_ref, far_ref, new_ref, up_ref, out_ref, latent_ref = refs
    pieces = [(g, 128 * i) for g, count in enumerate(counts) for i in range(count)]
    lat, width = near_ref.shape[0] - EXTRA, near_ref.shape[1]
    core = lax.rem(lax.axis_index("head"), 2)
    ctx = lax.axis_index("ctx")
    z, pair = lax.rem(ctx, NZ), ctx // NZ
    length = partner_length(near_ref)
    near_bias = key_bias(width, length - core * width)
    far_bias = key_bias(width, length - (1 - core) * width)
    first = 2 * SHARED
    partner_new = jnp.concatenate(
        [near_ref[lat : lat + 16, first : first + KVR], near_ref[lat + 16 : lat + 32, first : first + lat - KVR]],
        axis=1,
    )
    new_keys = jnp.concatenate([new_ref[...], partner_new], axis=0)
    lane = lax.broadcasted_iota(jnp.int32, (16, 32), 1)
    line = lax.broadcasted_iota(jnp.int32, (16, 32), 0)
    key_offsets = jnp.zeros((16, 32), jnp.int32)
    for k in range(32):
        side = pair if k < 16 else 1 - pair
        key_offsets = jnp.where(lane == k, offset_ref[(side * NZ + z) * 16 + k % 16], key_offsets)
    new_bias = []
    for block in range(NZ):
        first = (pair * NZ + lax.rem(z + OFFSETS[block], NZ)) * 16
        token_offsets = jnp.zeros((16, 32), jnp.int32)
        for t in range(16):
            token_offsets = jnp.where(line == t, offset_ref[first + t], token_offsets)
        new_bias.append(jnp.where(key_offsets <= token_offsets, 0.0, masked_value))
    wide = lax.broadcasted_iota(jnp.int32, (128, 128), 1)
    levels = jnp.zeros((128, 128), jnp.float32)
    for tile in range(NZ // 2):
        both = pieces[2 * tile : 2 * tile + 2]
        rows = jnp.concatenate([queries[2 * tile][...], queries[2 * tile + 1][...]], axis=0)
        stat = jnp.concatenate([states[2 * g + 1][r : r + 128, :] for g, r in both], axis=0)
        acc, high, total = fold(
            [
                dot_nn(rows, near_ref[0:lat, :]) + near_bias,
                dot_nn(rows, far_ref[0:lat, :]) + far_bias,
                dot_nt(rows, new_keys)
                + jnp.concatenate([new_bias[2 * tile]] * 8 + [new_bias[2 * tile + 1]] * 8, axis=0),
            ],
            [
                lambda w: dot_nt(w, near_ref[0:KVR, :]),
                lambda w: dot_nt(w, far_ref[0:KVR, :]),
                lambda w: dot_nn(w, new_keys[:, 0:KVR]),
            ],
            jnp.concatenate([states[2 * g][r : r + 128, :] for g, r in both], axis=0),
            stat[:, 0:1],
            stat[:, 1:2],
        )
        latent_ref[tile * 256 : (tile + 1) * 256, :] = (acc * (1.0 / total)).astype(jnp.bfloat16)
        level = high * exp_scale + jnp.log2(total)
        levels = jnp.where(wide == 2 * tile, level[:128], levels)
        levels = jnp.where(wide == 2 * tile + 1, level[128:], levels)
    slots = [lax.rem(z + OFFSETS[block], NZ) for block in range(NZ)]
    for head in range(8):
        latent = jnp.concatenate(
            [latent_ref[b * 128 + head * 16 : b * 128 + head * 16 + 16, :] for b in range(NZ)], axis=0
        )
        result = dot_nn(latent, up_ref[head]).astype(jnp.bfloat16)
        for block in range(NZ):
            out_ref[slots[block], head * 16 : head * 16 + 16, :] = result[block * 16 : block * 16 + 16]
    flat = levels.T
    p0 = flat.astype(jnp.bfloat16).astype(jnp.float32)
    p1 = (flat - p0).astype(jnp.bfloat16).astype(jnp.float32)
    p2 = flat - p0 - p1
    r = lax.broadcasted_iota(jnp.int32, (STAT, 128), 0)
    for block in range(NZ):
        stats = jnp.where(
            r == 0,
            p0[block : block + 1],
            jnp.where(r == 1, p1[block : block + 1], jnp.where(r == 2, p2[block : block + 1], 0.0)),
        )
        out_ref[slots[block], 128 : 128 + STAT, :] = stats.astype(jnp.bfloat16)


def merge_kernel(part_ref, out_ref, order_ref):
    levels = []
    for source in range(NZ):
        stats = part_ref[source, 128 : 128 + STAT, :].astype(jnp.float32)
        levels.append(stats[0:1] + stats[1:2] + stats[2:3])
    level = jnp.concatenate(levels, axis=0)
    factor = jnp.exp2(level - jnp.max(level, axis=0, keepdims=True))
    factor = factor / jnp.sum(factor, axis=0, keepdims=True)
    factor = jnp.concatenate([factor, jnp.zeros((128 - NZ, 128), jnp.float32)], axis=0).T
    total = jnp.zeros((128, VDIM), jnp.float32)
    for source in range(NZ):
        total = total + part_ref[source, 0:128, :].astype(jnp.float32) * factor[:, source : source + 1]
    for head in range(8):
        order_ref[pl.ds(head, 16, stride=8), :] = total[head * 16 : head * 16 + 16]
    out_ref[...] = order_ref[...].astype(jnp.bfloat16)


def shards(queries, cache, new_latents, cache_lengths, new_offsets, value_up_weight):
    own_tokens, head_local, lat = queries.shape
    rows = own_tokens * head_local
    z = lax.axis_index("ctx") % NZ
    keys = cache.T

    def across(a):
        moves = [
            (c * 16 + h, ((c + NZ) % 16) * 16 + (h + 8) % 16) for c in range(16) for h in range(16)
        ]
        return lax.ppermute(a, ("ctx", "head"), moves)

    def swap(a):
        return lax.ppermute(a, "head", [(h, h ^ 1) for h in range(16)])

    def shift(a, step):
        return lax.ppermute(
            a, "ctx", [(c, c // NZ * NZ + (c + step) % NZ) for c in range(16)]
        )

    width = cache.shape[0] // 2
    hbm = pl.BlockSpec(memory_space=pltpu.HBM)
    shared, direct, own = pl.pallas_call(
        pack_kernel,
        in_specs=[SMEM, hbm, hbm, hbm],
        out_specs=[hbm, hbm, VMEM],
        out_shape=[
            jax.ShapeDtypeStruct((lat, SHARED), jnp.bfloat16),
            jax.ShapeDtypeStruct((lat + EXTRA, width - 2 * SHARED), jnp.bfloat16),
            jax.ShapeDtypeStruct((rows, lat), jnp.bfloat16),
        ],
        scratch_shapes=[
            pltpu.VMEM((lat + EXTRA, width - SHARED), jnp.bfloat16),
            pltpu.VMEM((own_tokens, lat), jnp.bfloat16),
            pltpu.VMEM((own_tokens, head_local, lat), jnp.bfloat16),
            pltpu.VMEM((-(-lat // 128), rows, 128), jnp.float32),
            pltpu.SemaphoreType.DMA((6,)),
        ],
        compiler_params=pltpu.CompilerParams(vmem_limit_bytes=4 * 2**20),
        name="pack",
    )(
        cache_lengths,
        pltpu.with_memory_space_constraint(keys, pltpu.HBM),
        pltpu.with_memory_space_constraint(new_latents, pltpu.HBM),
        pltpu.with_memory_space_constraint(queries, pltpu.HBM),
    )
    mine = across(shared)

    state0 = attend_own(cache_lengths, [own], keys)
    up1, down1 = shift(own, 1), shift(own, -1)
    state0, direct = lax.optimization_barrier((state0, direct))
    direct = across(direct)
    up1, down1, state0 = lax.optimization_barrier((up1, down1, state0))
    up2, down2 = shift(up1, 1), shift(down1, -1)
    state1 = attend_own(cache_lengths, [up1, down1], keys)
    state1, mine = lax.optimization_barrier((state1, mine))
    other = lax.ppermute(mine, "head", [(h, h ^ 2) for h in range(16)])
    up2, down2, state1 = lax.optimization_barrier((up2, down2, state1))
    up3, down3 = shift(up2, 1), shift(down2, -1)
    four = lax.ppermute(
        jnp.where(z % 2 == 0, up2, down2),
        "ctx",
        [(c, c // NZ * NZ + (c + (2 if c % 2 == 0 else -2)) % NZ) for c in range(16)],
    )
    state2 = attend_own(cache_lengths, [up2, down2], keys)
    up3, down3, four, state2, other, direct = lax.optimization_barrier(
        (up3, down3, four, state2, other, direct)
    )
    near = pl.pallas_call(
        join_kernel,
        in_specs=[VMEM] * 3,
        out_specs=VMEM,
        out_shape=jax.ShapeDtypeStruct((lat + EXTRA, width), jnp.bfloat16),
        compiler_params=pltpu.CompilerParams(vmem_limit_bytes=6 * 2**20),
        cost_estimate=small_cost,
        name="join",
    )(mine, other, direct)
    far = swap(near)
    state3 = attend_own(cache_lengths, [up3, down3, four], keys)
    far, state3 = lax.optimization_barrier((far, state3))
    states = [part for state in (state0, state1, state2, state3) for part in state]
    parts = pl.pallas_call(
        functools.partial(final_kernel, [1, 2, 2, 3]),
        in_specs=[SMEM] + [VMEM] * (NZ + 12),
        out_specs=VMEM,
        out_shape=jax.ShapeDtypeStruct((NZ, rows + STAT, VDIM), jnp.bfloat16),
        scratch_shapes=[pltpu.VMEM((NZ * rows, KVR), jnp.bfloat16)],
        compiler_params=pltpu.CompilerParams(vmem_limit_bytes=16 * 2**20),
        cost_estimate=small_cost,
        name="attend_final",
    )(new_offsets, own, up1, down1, up2, down2, up3, down3, four, *states, near, far, new_latents, value_up_weight)
    got = lax.all_to_all(
        parts, "ctx", 0, 0, axis_index_groups=[[*range(NZ)], [*range(NZ, 2 * NZ)]], tiled=True
    )
    out = pl.pallas_call(
        merge_kernel,
        in_specs=[VMEM],
        out_specs=VMEM,
        out_shape=jax.ShapeDtypeStruct((rows, VDIM), jnp.bfloat16),
        scratch_shapes=[pltpu.VMEM((rows, VDIM), jnp.float32)],
        name="merge",
    )(pltpu.with_memory_space_constraint(got, pltpu.VMEM))
    return out.reshape(own_tokens, head_local, VDIM)


def solution(mesh):
    return jax.shard_map(
        shards,
        mesh=mesh,
        in_specs=(
            P("ctx", "head", None),
            P("ctx", None),
            P("ctx", None),
            P("ctx"),
            P(),
            P("head", None, None),
        ),
        out_specs=P("ctx", "head", None),
        check_vma=False,
    )
```

```python
import functools

import jax
import jax.numpy as jnp
from jax import lax
from jax.experimental import pallas as pl
from jax.experimental.pallas import tpu as pltpu
from jax.sharding import PartitionSpec as P

KVR = 512
VDIM = 128
EXTRA = 32
STAT = 16
NZ = 8
OFFSETS = [0, 7, 1, 6, 2, 5, 3, 4]
SHARED = 256

exp_scale = 192.0 ** (-0.5) * 1.4426950408889634
masked_value = -1e30
NT = (((1,), (1,)), ((), ()))
small_cost = pl.CostEstimate(flops=10**6, bytes_accessed=10**4, transcendentals=0)
VMEM = pl.BlockSpec(memory_space=pltpu.VMEM)
SMEM = pl.BlockSpec(memory_space=pltpu.SMEM)


def dot_nt(a, b):
    return lax.dot_general(a, b, NT, preferred_element_type=jnp.float32)


def dot_nn(a, b):
    return jnp.dot(a, b, preferred_element_type=jnp.float32)


def pack_stats(high, total):
    lane = lax.broadcasted_iota(jnp.int32, (high.shape[0], 128), 1)
    return jnp.where(lane == 0, high, total)


def key_bias(width, valid):
    position = lax.broadcasted_iota(jnp.int32, (1, width), 1)
    return jnp.where(position < valid, 0.0, masked_value)


def pack_kernel(len_ref, keys_ref, new_ref, shared_ref, direct_ref, stage_ref, new_vmem, sems):
    head = lax.axis_index("head")
    core, side = lax.rem(head, 2), lax.rem(head // 2, 2)
    lat, few = shared_ref.shape
    width = direct_ref.shape[1]
    early, late = few // 128, width // 128

    def load(run, slot):
        place = pl.multiple_of((2 * run + core) * 128, 128)
        return pltpu.make_async_copy(
            keys_ref.at[:, pl.ds(place, 128)],
            stage_ref.at[0:lat, slot * 128 : (slot + 1) * 128],
            sems.at[slot],
        )

    loads = [load(side * early + i, i) for i in range(early)]
    loads += [load(2 * early + i, early + i) for i in range(late)]
    load_new = pltpu.make_async_copy(new_ref, new_vmem, sems.at[early + late])
    send_shared = pltpu.make_async_copy(
        stage_ref.at[0:lat, 0:few], shared_ref, sems.at[early + late + 1]
    )
    send_direct = pltpu.make_async_copy(
        stage_ref.at[:, few : few + width], direct_ref, sems.at[early + late + 2]
    )
    for copy in loads[:early] + [load_new] + loads[early:]:
        copy.start()
    length = len_ref[0]
    high = length // 256
    r = lax.broadcasted_iota(jnp.int32, (16, 128), 0)
    c = lax.broadcasted_iota(jnp.int32, (16, 128), 1)
    note = jnp.where(
        (r == 0) & (c == 0), high, jnp.where((r == 0) & (c == 1), length - high * 256, 0)
    ).astype(jnp.float32)
    stage_ref[lat + 16 : lat + 32, few + 128 : few + 256] = note.astype(jnp.bfloat16)
    for copy in loads[:early]:
        copy.wait()
    send_shared.start()
    load_new.wait()
    stage_ref[lat : lat + 16, few : few + KVR] = new_vmem[:, 0:KVR]
    stage_ref[lat + 16 : lat + 32, few : few + lat - KVR] = new_vmem[:, KVR:lat]
    for copy in loads[early:]:
        copy.wait()
    send_direct.start()
    send_shared.wait()
    send_direct.wait()


def join_kernel(mine_ref, other_ref, direct_ref, near_ref):
    side = lax.rem(lax.axis_index("head") // 2, 2)
    lat, few = mine_ref.shape
    near_ref[0:lat, pl.ds(pl.multiple_of(side * few, 128), few)] = mine_ref[...]
    near_ref[0:lat, pl.ds(pl.multiple_of((1 - side) * few, 128), few)] = other_ref[...]
    near_ref[:, 2 * few :] = direct_ref[...]
    near_ref[lat:, 0 : 2 * few] = jnp.zeros((EXTRA, 2 * few), jnp.bfloat16)


def run_bias(width, core, valid):
    lane = lax.broadcasted_iota(jnp.int32, (1, width), 1)
    return jnp.where(lane + (lane // 128 + core) * 128 < valid, 0.0, masked_value)


def own_kernel(blocks, len_ref, *refs):
    query_refs, (keys_ref, acc_ref, stat_ref) = refs[:blocks], refs[blocks:]
    valid = len_ref[0]
    full = keys_ref.shape[1]
    widths = [full // 2, full * 3 // 4, full]

    def attend(width):
        rows = jnp.concatenate([r[...] for r in query_refs], axis=0)
        scores = dot_nn(rows, keys_ref[:, 0:width]) + key_bias(width, valid)
        high = jnp.max(scores, axis=1, keepdims=True)
        weights = jnp.exp2((scores - high) * exp_scale)
        total = jnp.sum(weights, axis=1, keepdims=True)
        acc_ref[...] = dot_nt(weights.astype(jnp.bfloat16), keys_ref[0:KVR, 0:width])
        stat_ref[...] = pack_stats(high, total)

    least = 0
    for width in widths:
        pl.when((valid > least) & (valid <= width))(functools.partial(attend, width))
        least = width


def attend_own(valid, blocks, keys):
    rows = sum(b.shape[0] for b in blocks)
    width = keys.shape[1]
    return pl.pallas_call(
        functools.partial(own_kernel, len(blocks)),
        in_specs=[SMEM] + [VMEM] * (len(blocks) + 1),
        out_specs=[VMEM, VMEM],
        out_shape=[
            jax.ShapeDtypeStruct((rows, KVR), jnp.float32),
            jax.ShapeDtypeStruct((rows, 128), jnp.float32),
        ],
        compiler_params=pltpu.CompilerParams(vmem_limit_bytes=12 * 2**20),
        cost_estimate=small_cost,
        name="attend_own",
    )(valid, *blocks, keys)


def partner_length(part_ref):
    lat = part_ref.shape[0] - EXTRA
    row = part_ref[lat + 16 : lat + 32, 2 * SHARED + 128 : 2 * SHARED + 256].astype(jnp.float32)
    r = lax.broadcasted_iota(jnp.int32, row.shape, 0)
    c = lax.broadcasted_iota(jnp.int32, row.shape, 1)
    high = jnp.sum(jnp.where((r == 0) & (c == 0), row, 0.0))
    low = jnp.sum(jnp.where((r == 0) & (c == 1), row, 0.0))
    return (high * 256.0 + low).astype(jnp.int32)


def fold(scores, values, acc, high, total):
    new_high = functools.reduce(
        jnp.maximum, [jnp.max(s, axis=1, keepdims=True) for s in scores], high
    )
    rescale = jnp.exp2((high - new_high) * exp_scale)
    acc = acc * rescale
    total = total * rescale
    for s, v in zip(scores, values):
        weights = jnp.exp2((s - new_high) * exp_scale)
        total = total + jnp.sum(weights, axis=1, keepdims=True)
        acc = acc + v(weights.astype(jnp.bfloat16))
    return acc, new_high, total


def final_kernel(counts, offset_ref, *refs):
    queries, refs = refs[:NZ], refs[NZ:]
    states, refs = refs[: 2 * len(counts)], refs[2 * len(counts) :]
    near_ref, far_ref, new_ref, up_ref, out_ref, latent_ref = refs
    pieces = [(g, 128 * i) for g, count in enumerate(counts) for i in range(count)]
    lat, width = near_ref.shape[0] - EXTRA, near_ref.shape[1]
    core = lax.rem(lax.axis_index("head"), 2)
    ctx = lax.axis_index("ctx")
    z, pair = lax.rem(ctx, NZ), ctx // NZ
    length = partner_length(near_ref)
    near_bias, far_bias = run_bias(width, core, length), run_bias(width, 1 - core, length)
    start = 2 * SHARED
    partner_new = jnp.concatenate(
        [near_ref[lat : lat + 16, start : start + KVR], near_ref[lat + 16 : lat + 32, start : start + lat - KVR]],
        axis=1,
    )
    new_keys = jnp.concatenate([new_ref[...], partner_new], axis=0)
    lane = lax.broadcasted_iota(jnp.int32, (8, 32), 1)
    key_offsets = jnp.zeros((8, 32), jnp.int32)
    for k in range(32):
        side = pair if k < 16 else 1 - pair
        key_offsets = jnp.where(lane == k, offset_ref[(side * NZ + z) * 16 + k % 16], key_offsets)
    to_row = lax.broadcasted_iota(jnp.int32, (256, 256), 0)
    from_row = lax.broadcasted_iota(jnp.int32, (256, 256), 1)
    source = to_row // 128 * 128 + to_row % 16 * 8 + to_row % 128 // 16
    reorder = jnp.where(from_row == source, 1.0, 0.0).astype(jnp.bfloat16)
    wide = lax.broadcasted_iota(jnp.int32, (128, 128), 1)
    levels = jnp.zeros((128, 128), jnp.float32)
    for tile in range(NZ // 2):
        both = pieces[2 * tile : 2 * tile + 2]
        rows = jnp.concatenate([queries[2 * tile][...], queries[2 * tile + 1][...]], axis=0)
        stat = jnp.concatenate([states[2 * g + 1][r : r + 128, :] for g, r in both], axis=0)
        new_bias = []
        for block in (2 * tile, 2 * tile + 1):
            token = (pair * NZ + lax.rem(z + OFFSETS[block], NZ)) * 16
            new_bias += [
                jnp.where(key_offsets <= offset_ref[token + t], 0.0, masked_value) for t in range(16)
            ]
        acc, high, total = fold(
            [
                dot_nn(rows, near_ref[0:lat, :]) + near_bias,
                dot_nn(rows, far_ref[0:lat, :]) + far_bias,
                dot_nt(rows, new_keys) + jnp.concatenate(new_bias, axis=0),
            ],
            [
                lambda w: dot_nt(w, near_ref[0:KVR, :]),
                lambda w: dot_nt(w, far_ref[0:KVR, :]),
                lambda w: dot_nn(w, new_keys[:, 0:KVR]),
            ],
            jnp.concatenate([states[2 * g][r : r + 128, :] for g, r in both], axis=0),
            stat[:, 0:1],
            stat[:, 1:2],
        )
        latent = (acc * (1.0 / total)).astype(jnp.bfloat16)
        latent_ref[tile * 256 : (tile + 1) * 256, :] = dot_nn(reorder, latent).astype(jnp.bfloat16)
        level = high * exp_scale + jnp.log2(total)
        levels = jnp.where(wide == 2 * tile, level[:128], levels)
        levels = jnp.where(wide == 2 * tile + 1, level[128:], levels)
    slots = [lax.rem(z + OFFSETS[block], NZ) for block in range(NZ)]
    for head in range(8):
        latent = jnp.concatenate(
            [latent_ref[b * 128 + head * 16 : b * 128 + head * 16 + 16, :] for b in range(NZ)], axis=0
        )
        result = dot_nn(latent, up_ref[head]).astype(jnp.bfloat16)
        for block in range(NZ):
            out_ref[slots[block], head * 16 : head * 16 + 16, :] = result[block * 16 : block * 16 + 16]
    flat = levels.T
    p0 = flat.astype(jnp.bfloat16).astype(jnp.float32)
    p1 = (flat - p0).astype(jnp.bfloat16).astype(jnp.float32)
    p2 = flat - p0 - p1
    r = lax.broadcasted_iota(jnp.int32, (STAT, 128), 0)
    for block in range(NZ):
        stats = jnp.where(
            r == 0,
            p0[block : block + 1],
            jnp.where(r == 1, p1[block : block + 1], jnp.where(r == 2, p2[block : block + 1], 0.0)),
        )
        out_ref[slots[block], 128 : 128 + STAT, :] = stats.astype(jnp.bfloat16)


def merge_kernel(part_ref, out_ref, order_ref):
    levels = []
    for source in range(NZ):
        stats = part_ref[source, 128 : 128 + STAT, :].astype(jnp.float32)
        levels.append(stats[0:1] + stats[1:2] + stats[2:3])
    level = jnp.concatenate(levels, axis=0)
    factor = jnp.exp2(level - jnp.max(level, axis=0, keepdims=True))
    factor = factor / jnp.sum(factor, axis=0, keepdims=True)
    order_ref[...] = jnp.concatenate([factor, jnp.zeros((128 - NZ, 128), jnp.float32)], axis=0).T
    factor = jnp.concatenate([order_ref[pl.ds(head, 16, stride=8), :] for head in range(8)], axis=0)
    total = jnp.zeros((128, VDIM), jnp.float32)
    for source in range(NZ):
        total = total + part_ref[source, 0:128, :].astype(jnp.float32) * factor[:, source : source + 1]
    for head in range(8):
        order_ref[pl.ds(head, 16, stride=8), :] = total[head * 16 : head * 16 + 16]
    out_ref[...] = order_ref[...].astype(jnp.bfloat16)


def shards(queries, cache, new_latents, cache_lengths, new_offsets, value_up_weight):
    own_tokens, head_local, lat = queries.shape
    rows = own_tokens * head_local
    z = lax.axis_index("ctx") % NZ
    keys = cache.T

    def across(a):
        moves = [
            (c * 16 + h, ((c + NZ) % 16) * 16 + (h + 8) % 16) for c in range(16) for h in range(16)
        ]
        return lax.ppermute(a, ("ctx", "head"), moves)

    def swap(a):
        return lax.ppermute(a, "head", [(h, h ^ 1) for h in range(16)])

    def shift(a, step):
        return lax.ppermute(
            a, "ctx", [(c, c // NZ * NZ + (c + step) % NZ) for c in range(16)]
        )

    own = queries.reshape(rows, lat)
    up1, down1 = shift(own, 1), shift(own, -1)

    width = cache.shape[0] // 2
    hbm = pl.BlockSpec(memory_space=pltpu.HBM)
    shared, direct = pl.pallas_call(
        pack_kernel,
        in_specs=[SMEM, hbm, hbm],
        out_specs=[hbm, hbm],
        out_shape=[
            jax.ShapeDtypeStruct((lat, SHARED), jnp.bfloat16),
            jax.ShapeDtypeStruct((lat + EXTRA, width - 2 * SHARED), jnp.bfloat16),
        ],
        scratch_shapes=[
            pltpu.VMEM((lat + EXTRA, width - SHARED), jnp.bfloat16),
            pltpu.VMEM((own_tokens, lat), jnp.bfloat16),
            pltpu.SemaphoreType.DMA(((width - SHARED) // 128 + 3,)),
        ],
        compiler_params=pltpu.CompilerParams(vmem_limit_bytes=4 * 2**20),
        name="pack",
    )(
        cache_lengths,
        pltpu.with_memory_space_constraint(keys, pltpu.HBM),
        pltpu.with_memory_space_constraint(new_latents, pltpu.HBM),
    )
    mine, direct = across(shared), across(direct)

    up1, down1 = lax.optimization_barrier((up1, down1))
    up2, down2 = shift(up1, 1), shift(down1, -1)
    state1 = attend_own(cache_lengths, [own, up1, down1], keys)
    state1, mine = lax.optimization_barrier((state1, mine))
    other = lax.ppermute(mine, "head", [(h, h ^ 2) for h in range(16)])
    up2, down2, state1 = lax.optimization_barrier((up2, down2, state1))
    up3, down3 = shift(up2, 1), shift(down2, -1)
    four = lax.ppermute(
        jnp.where(z % 2 == 0, up2, down2),
        "ctx",
        [(c, c // NZ * NZ + (c + (2 if c % 2 == 0 else -2)) % NZ) for c in range(16)],
    )
    state2 = attend_own(cache_lengths, [up2, down2], keys)
    up3, down3, four, state2, other, direct = lax.optimization_barrier(
        (up3, down3, four, state2, other, direct)
    )
    near = pl.pallas_call(
        join_kernel,
        in_specs=[VMEM] * 3,
        out_specs=VMEM,
        out_shape=jax.ShapeDtypeStruct((lat + EXTRA, width), jnp.bfloat16),
        compiler_params=pltpu.CompilerParams(vmem_limit_bytes=6 * 2**20),
        cost_estimate=small_cost,
        name="join",
    )(mine, other, pltpu.with_memory_space_constraint(direct, pltpu.VMEM))
    far = swap(near)
    state3 = attend_own(cache_lengths, [up3, down3, four], keys)
    far, state3 = lax.optimization_barrier((far, state3))
    states = [part for state in (state1, state2, state3) for part in state]
    parts = pl.pallas_call(
        functools.partial(final_kernel, [3, 2, 3]),
        in_specs=[SMEM] + [VMEM] * (NZ + 10),
        out_specs=VMEM,
        out_shape=jax.ShapeDtypeStruct((NZ, rows + STAT, VDIM), jnp.bfloat16),
        scratch_shapes=[pltpu.VMEM((NZ * rows, KVR), jnp.bfloat16)],
        compiler_params=pltpu.CompilerParams(vmem_limit_bytes=16 * 2**20),
        cost_estimate=small_cost,
        name="attend_final",
    )(new_offsets, own, up1, down1, up2, down2, up3, down3, four, *states, near, far, new_latents, value_up_weight)
    got = lax.all_to_all(
        parts, "ctx", 0, 0, axis_index_groups=[[*range(NZ)], [*range(NZ, 2 * NZ)]], tiled=True
    )
    out = pl.pallas_call(
        merge_kernel,
        in_specs=[VMEM],
        out_specs=VMEM,
        out_shape=jax.ShapeDtypeStruct((rows, VDIM), jnp.bfloat16),
        scratch_shapes=[pltpu.VMEM((rows, VDIM), jnp.float32)],
        name="merge",
    )(pltpu.with_memory_space_constraint(got, pltpu.VMEM))
    return out.reshape(own_tokens, head_local, VDIM)


def solution(mesh):
    return jax.shard_map(
        shards,
        mesh=mesh,
        in_specs=(
            P("ctx", "head", None),
            P("ctx", None),
            P("ctx", None),
            P("ctx"),
            P(),
            P("head", None, None),
        ),
        out_specs=P("ctx", "head", None),
        check_vma=False,
    )
```

```python
import functools

import jax
import jax.numpy as jnp
from jax import lax
from jax.experimental import pallas as pl
from jax.experimental.pallas import tpu as pltpu
from jax.sharding import PartitionSpec as P

KVR = 512
VDIM = 128
EXTRA = 32
STAT = 16
NZ = 8
OFFSETS = [0, 7, 1, 6, 2, 5, 3, 4]
SHARED = 256

exp_scale = 192.0 ** (-0.5) * 1.4426950408889634
masked_value = -1e30
NT = (((1,), (1,)), ((), ()))
small_cost = pl.CostEstimate(flops=10**6, bytes_accessed=10**4, transcendentals=0)
VMEM = pl.BlockSpec(memory_space=pltpu.VMEM)
SMEM = pl.BlockSpec(memory_space=pltpu.SMEM)


def dot_nt(a, b):
    return lax.dot_general(a, b, NT, preferred_element_type=jnp.float32)


def dot_nn(a, b):
    return jnp.dot(a, b, preferred_element_type=jnp.float32)


def pack_stats(high, total):
    lane = lax.broadcasted_iota(jnp.int32, (high.shape[0], 128), 1)
    return jnp.where(lane == 0, high, total)


def key_bias(width, valid):
    position = lax.broadcasted_iota(jnp.int32, (1, width), 1)
    return jnp.where(position < valid, 0.0, masked_value)


def pack_kernel(len_ref, keys_ref, new_ref, shared_ref, direct_ref, stage_ref, new_vmem, sems):
    head = lax.axis_index("head")
    core, side = lax.rem(head, 2), lax.rem(head // 2, 2)
    lat, few = shared_ref.shape
    width = direct_ref.shape[1]
    early, late = few // 128, width // 128

    def load(run, slot):
        place = pl.multiple_of((2 * run + core) * 128, 128)
        return pltpu.make_async_copy(
            keys_ref.at[:, pl.ds(place, 128)],
            stage_ref.at[0:lat, slot * 128 : (slot + 1) * 128],
            sems.at[slot],
        )

    loads = [load(side * early + i, i) for i in range(early)]
    loads += [load(2 * early + i, early + i) for i in range(late)]
    load_new = pltpu.make_async_copy(new_ref, new_vmem, sems.at[early + late])
    send_shared = pltpu.make_async_copy(
        stage_ref.at[0:lat, 0:few], shared_ref, sems.at[early + late + 1]
    )
    send_direct = pltpu.make_async_copy(
        stage_ref.at[:, few : few + width], direct_ref, sems.at[early + late + 2]
    )
    for copy in loads[:early] + [load_new] + loads[early:]:
        copy.start()
    length = len_ref[0]
    high = length // 256
    r = lax.broadcasted_iota(jnp.int32, (16, 128), 0)
    c = lax.broadcasted_iota(jnp.int32, (16, 128), 1)
    note = jnp.where(
        (r == 0) & (c == 0), high, jnp.where((r == 0) & (c == 1), length - high * 256, 0)
    ).astype(jnp.float32)
    stage_ref[lat + 16 : lat + 32, few + 128 : few + 256] = note.astype(jnp.bfloat16)
    for copy in loads[:early]:
        copy.wait()
    send_shared.start()
    load_new.wait()
    stage_ref[lat : lat + 16, few : few + KVR] = new_vmem[:, 0:KVR]
    stage_ref[lat + 16 : lat + 32, few : few + lat - KVR] = new_vmem[:, KVR:lat]
    for copy in loads[early:]:
        copy.wait()
    send_direct.start()
    send_shared.wait()
    send_direct.wait()


def run_bias(width, first, core, valid):
    lane = lax.broadcasted_iota(jnp.int32, (1, width), 1)
    position = lane + lane // 128 * 128 + 2 * first + core * 128
    return jnp.where(position < valid, 0.0, masked_value)


def own_kernel(blocks, len_ref, *refs):
    query_refs, (keys_ref, acc_ref, stat_ref) = refs[:blocks], refs[blocks:]
    valid = len_ref[0]
    full = keys_ref.shape[1]
    widths = [full // 2, full * 3 // 4, full]

    def attend(width):
        rows = jnp.concatenate([r[...] for r in query_refs], axis=0)
        scores = dot_nn(rows, keys_ref[:, 0:width]) + key_bias(width, valid)
        high = jnp.max(scores, axis=1, keepdims=True)
        weights = jnp.exp2((scores - high) * exp_scale)
        total = jnp.sum(weights, axis=1, keepdims=True)
        acc_ref[...] = dot_nt(weights.astype(jnp.bfloat16), keys_ref[0:KVR, 0:width])
        stat_ref[...] = pack_stats(high, total)

    least = 0
    for width in widths:
        pl.when((valid > least) & (valid <= width))(functools.partial(attend, width))
        least = width


def attend_own(valid, blocks, keys):
    rows = sum(b.shape[0] for b in blocks)
    width = keys.shape[1]
    return pl.pallas_call(
        functools.partial(own_kernel, len(blocks)),
        in_specs=[SMEM] + [VMEM] * (len(blocks) + 1),
        out_specs=[VMEM, VMEM],
        out_shape=[
            jax.ShapeDtypeStruct((rows, KVR), jnp.float32),
            jax.ShapeDtypeStruct((rows, 128), jnp.float32),
        ],
        compiler_params=pltpu.CompilerParams(vmem_limit_bytes=12 * 2**20),
        cost_estimate=small_cost,
        name="attend_own",
    )(valid, *blocks, keys)


def partner_length(part_ref):
    lat = part_ref.shape[0] - EXTRA
    row = part_ref[lat + 16 : lat + 32, 128:256].astype(jnp.float32)
    r = lax.broadcasted_iota(jnp.int32, row.shape, 0)
    c = lax.broadcasted_iota(jnp.int32, row.shape, 1)
    high = jnp.sum(jnp.where((r == 0) & (c == 0), row, 0.0))
    low = jnp.sum(jnp.where((r == 0) & (c == 1), row, 0.0))
    return (high * 256.0 + low).astype(jnp.int32)


def fold(scores, values, acc, high, total):
    new_high = functools.reduce(
        jnp.maximum, [jnp.max(s, axis=1, keepdims=True) for s in scores], high
    )
    rescale = jnp.exp2((high - new_high) * exp_scale)
    acc = acc * rescale
    total = total * rescale
    for s, v in zip(scores, values):
        weights = jnp.exp2((s - new_high) * exp_scale)
        total = total + jnp.sum(weights, axis=1, keepdims=True)
        acc = acc + v(weights.astype(jnp.bfloat16))
    return acc, new_high, total


def final_kernel(counts, offset_ref, *refs):
    queries, refs = refs[:NZ], refs[NZ:]
    states, refs = refs[: 2 * len(counts)], refs[2 * len(counts) :]
    parts, (new_ref, up_ref, out_ref, latent_ref) = refs[:6], refs[6:]
    pieces = [(g, 128 * i) for g, count in enumerate(counts) for i in range(count)]
    mine_ref, direct_ref = parts[0], parts[2]
    lat = mine_ref.shape[0]
    head = lax.axis_index("head")
    core, side = lax.rem(head, 2), lax.rem(head // 2, 2)
    ctx = lax.axis_index("ctx")
    z, pair = lax.rem(ctx, NZ), ctx // NZ
    length = partner_length(direct_ref)
    firsts = [side * SHARED, (1 - side) * SHARED, 2 * SHARED]
    biases = [
        run_bias(parts[3 * i + j].shape[1], firsts[j], core if i == 0 else 1 - core, length)
        for i in range(2)
        for j in range(3)
    ]

    def values_of(ref):
        return lambda w: dot_nt(w, ref[0:KVR, :])

    partner_new = jnp.concatenate(
        [direct_ref[lat : lat + 16, 0:KVR], direct_ref[lat + 16 : lat + 32, 0 : lat - KVR]], axis=1
    )
    new_keys = jnp.concatenate([new_ref[...], partner_new], axis=0)
    lane = lax.broadcasted_iota(jnp.int32, (8, 32), 1)
    key_offsets = jnp.zeros((8, 32), jnp.int32)
    for k in range(32):
        side = pair if k < 16 else 1 - pair
        key_offsets = jnp.where(lane == k, offset_ref[(side * NZ + z) * 16 + k % 16], key_offsets)
    to_row = lax.broadcasted_iota(jnp.int32, (256, 256), 0)
    from_row = lax.broadcasted_iota(jnp.int32, (256, 256), 1)
    source = to_row // 128 * 128 + to_row % 16 * 8 + to_row % 128 // 16
    reorder = jnp.where(from_row == source, 1.0, 0.0).astype(jnp.bfloat16)
    wide = lax.broadcasted_iota(jnp.int32, (128, 128), 1)
    levels = jnp.zeros((128, 128), jnp.float32)
    for tile in range(NZ // 2):
        both = pieces[2 * tile : 2 * tile + 2]
        rows = jnp.concatenate([queries[2 * tile][...], queries[2 * tile + 1][...]], axis=0)
        stat = jnp.concatenate([states[2 * g + 1][r : r + 128, :] for g, r in both], axis=0)
        new_bias = []
        for block in (2 * tile, 2 * tile + 1):
            token = (pair * NZ + lax.rem(z + OFFSETS[block], NZ)) * 16
            new_bias += [
                jnp.where(key_offsets <= offset_ref[token + t], 0.0, masked_value) for t in range(16)
            ]
        acc, high, total = fold(
            [dot_nn(rows, ref[0:lat, :]) + bias for ref, bias in zip(parts, biases)]
            + [dot_nt(rows, new_keys) + jnp.concatenate(new_bias, axis=0)],
            [values_of(ref) for ref in parts] + [lambda w: dot_nn(w, new_keys[:, 0:KVR])],
            jnp.concatenate([states[2 * g][r : r + 128, :] for g, r in both], axis=0),
            stat[:, 0:1],
            stat[:, 1:2],
        )
        latent = (acc * (1.0 / total)).astype(jnp.bfloat16)
        latent_ref[tile * 256 : (tile + 1) * 256, :] = dot_nn(reorder, latent).astype(jnp.bfloat16)
        level = high * exp_scale + jnp.log2(total)
        levels = jnp.where(wide == 2 * tile, level[:128], levels)
        levels = jnp.where(wide == 2 * tile + 1, level[128:], levels)
    slots = [lax.rem(z + OFFSETS[block], NZ) for block in range(NZ)]
    for head in range(8):
        latent = jnp.concatenate(
            [latent_ref[b * 128 + head * 16 : b * 128 + head * 16 + 16, :] for b in range(NZ)], axis=0
        )
        result = dot_nn(latent, up_ref[head]).astype(jnp.bfloat16)
        for block in range(NZ):
            out_ref[slots[block], head * 16 : head * 16 + 16, :] = result[block * 16 : block * 16 + 16]
    flat = levels.T
    p0 = flat.astype(jnp.bfloat16).astype(jnp.float32)
    p1 = (flat - p0).astype(jnp.bfloat16).astype(jnp.float32)
    p2 = flat - p0 - p1
    r = lax.broadcasted_iota(jnp.int32, (STAT, 128), 0)
    for block in range(NZ):
        stats = jnp.where(
            r == 0,
            p0[block : block + 1],
            jnp.where(r == 1, p1[block : block + 1], jnp.where(r == 2, p2[block : block + 1], 0.0)),
        )
        out_ref[slots[block], 128 : 128 + STAT, :] = stats.astype(jnp.bfloat16)


def merge_kernel(part_ref, out_ref, order_ref):
    levels = []
    for source in range(NZ):
        stats = part_ref[source, 128 : 128 + STAT, :].astype(jnp.float32)
        levels.append(stats[0:1] + stats[1:2] + stats[2:3])
    level = jnp.concatenate(levels, axis=0)
    factor = jnp.exp2(level - jnp.max(level, axis=0, keepdims=True))
    factor = factor / jnp.sum(factor, axis=0, keepdims=True)
    order_ref[...] = jnp.concatenate([factor, jnp.zeros((128 - NZ, 128), jnp.float32)], axis=0).T
    factor = jnp.concatenate([order_ref[pl.ds(head, 16, stride=8), :] for head in range(8)], axis=0)
    total = jnp.zeros((128, VDIM), jnp.float32)
    for source in range(NZ):
        total = total + part_ref[source, 0:128, :].astype(jnp.float32) * factor[:, source : source + 1]
    for head in range(8):
        order_ref[pl.ds(head, 16, stride=8), :] = total[head * 16 : head * 16 + 16]
    out_ref[...] = order_ref[...].astype(jnp.bfloat16)


def shards(queries, cache, new_latents, cache_lengths, new_offsets, value_up_weight):
    own_tokens, head_local, lat = queries.shape
    rows = own_tokens * head_local
    z = lax.axis_index("ctx") % NZ
    keys = cache.T

    def across(a):
        moves = [
            (c * 16 + h, ((c + NZ) % 16) * 16 + (h + 8) % 16) for c in range(16) for h in range(16)
        ]
        return lax.ppermute(a, ("ctx", "head"), moves)

    def swap(a):
        return lax.ppermute(a, "head", [(h, h ^ 1) for h in range(16)])

    def shift(a, step):
        return lax.ppermute(
            a, "ctx", [(c, c // NZ * NZ + (c + step) % NZ) for c in range(16)]
        )

    own = queries.reshape(rows, lat)
    up1, down1 = shift(own, 1), shift(own, -1)

    width = cache.shape[0] // 2
    hbm = pl.BlockSpec(memory_space=pltpu.HBM)
    shared, direct = pl.pallas_call(
        pack_kernel,
        in_specs=[SMEM, hbm, hbm],
        out_specs=[hbm, hbm],
        out_shape=[
            jax.ShapeDtypeStruct((lat, SHARED), jnp.bfloat16),
            jax.ShapeDtypeStruct((lat + EXTRA, width - 2 * SHARED), jnp.bfloat16),
        ],
        scratch_shapes=[
            pltpu.VMEM((lat + EXTRA, width - SHARED), jnp.bfloat16),
            pltpu.VMEM((own_tokens, lat), jnp.bfloat16),
            pltpu.SemaphoreType.DMA(((width - SHARED) // 128 + 3,)),
        ],
        compiler_params=pltpu.CompilerParams(vmem_limit_bytes=4 * 2**20),
        name="pack",
    )(
        cache_lengths,
        pltpu.with_memory_space_constraint(keys, pltpu.HBM),
        pltpu.with_memory_space_constraint(new_latents, pltpu.HBM),
    )
    mine, direct = across(shared), across(direct)

    up1, down1 = lax.optimization_barrier((up1, down1))
    up2, down2 = shift(up1, 1), shift(down1, -1)
    state1 = attend_own(cache_lengths, [own, up1, down1], keys)
    state1, mine = lax.optimization_barrier((state1, mine))
    other = lax.ppermute(mine, "head", [(h, h ^ 2) for h in range(16)])
    up2, down2, state1 = lax.optimization_barrier((up2, down2, state1))
    up3, down3 = shift(up2, 1), shift(down2, -1)
    four = lax.ppermute(
        jnp.where(z % 2 == 0, up2, down2),
        "ctx",
        [(c, c // NZ * NZ + (c + (2 if c % 2 == 0 else -2)) % NZ) for c in range(16)],
    )
    state2 = attend_own(cache_lengths, [up2, down2], keys)
    up3, down3, four, state2, mine, other, direct = lax.optimization_barrier(
        (up3, down3, four, state2, mine, other, direct)
    )
    far_mine, far_other, far_direct = swap(mine), swap(other), swap(direct)
    state3 = attend_own(cache_lengths, [up3, down3, four], keys)
    far_mine, far_other, far_direct, state3 = lax.optimization_barrier((far_mine, far_other, far_direct, state3))
    states = [part for state in (state1, state2, state3) for part in state]
    parts = pl.pallas_call(
        functools.partial(final_kernel, [3, 2, 3]),
        in_specs=[SMEM] + [VMEM] * (NZ + 14),
        out_specs=VMEM,
        out_shape=jax.ShapeDtypeStruct((NZ, rows + STAT, VDIM), jnp.bfloat16),
        scratch_shapes=[pltpu.VMEM((NZ * rows, KVR), jnp.bfloat16)],
        compiler_params=pltpu.CompilerParams(vmem_limit_bytes=16 * 2**20),
        cost_estimate=small_cost,
        name="attend_final",
    )(new_offsets, own, up1, down1, up2, down2, up3, down3, four, *states, mine, other, direct, far_mine, far_other, far_direct, new_latents, value_up_weight)
    got = lax.all_to_all(
        parts, "ctx", 0, 0, axis_index_groups=[[*range(NZ)], [*range(NZ, 2 * NZ)]], tiled=True
    )
    out = pl.pallas_call(
        merge_kernel,
        in_specs=[VMEM],
        out_specs=VMEM,
        out_shape=jax.ShapeDtypeStruct((rows, VDIM), jnp.bfloat16),
        scratch_shapes=[pltpu.VMEM((rows, VDIM), jnp.float32)],
        name="merge",
    )(pltpu.with_memory_space_constraint(got, pltpu.VMEM))
    return out.reshape(own_tokens, head_local, VDIM)


def solution(mesh):
    return jax.shard_map(
        shards,
        mesh=mesh,
        in_specs=(
            P("ctx", "head", None),
            P("ctx", None),
            P("ctx", None),
            P("ctx"),
            P(),
            P("head", None, None),
        ),
        out_specs=P("ctx", "head", None),
        check_vma=False,
    )
```

```python
import functools

import jax
import jax.numpy as jnp
from jax import lax
from jax.experimental import pallas as pl
from jax.experimental.pallas import tpu as pltpu
from jax.sharding import PartitionSpec as P

KVR = 512
VDIM = 128
EXTRA = 32
STAT = 16
NZ = 8
OFFSETS = [0, 7, 1, 6, 2, 5, 3, 4]
SHARED = 256

exp_scale = 192.0 ** (-0.5) * 1.4426950408889634
masked_value = -1e30
NT = (((1,), (1,)), ((), ()))
small_cost = pl.CostEstimate(flops=10**6, bytes_accessed=10**4, transcendentals=0)
VMEM = pl.BlockSpec(memory_space=pltpu.VMEM)
SMEM = pl.BlockSpec(memory_space=pltpu.SMEM)


def dot_nt(a, b):
    return lax.dot_general(a, b, NT, preferred_element_type=jnp.float32)


def dot_nn(a, b):
    return jnp.dot(a, b, preferred_element_type=jnp.float32)


def pack_stats(high, total):
    lane = lax.broadcasted_iota(jnp.int32, (high.shape[0], 128), 1)
    return jnp.where(lane == 0, high, total)


def key_bias(width, valid):
    position = lax.broadcasted_iota(jnp.int32, (1, width), 1)
    return jnp.where(position < valid, 0.0, masked_value)


def pack_kernel(len_ref, keys_ref, new_ref, shared_ref, direct_ref, stage_ref, new_vmem, sems):
    head = lax.axis_index("head")
    core, side = lax.rem(head, 2), lax.rem(head // 2, 2)
    lat, few = shared_ref.shape
    width = direct_ref.shape[1]
    early, late = few // 128, width // 128

    def load(run, slot):
        place = pl.multiple_of((2 * run + core) * 128, 128)
        return pltpu.make_async_copy(
            keys_ref.at[:, pl.ds(place, 128)],
            stage_ref.at[0:lat, slot * 128 : (slot + 1) * 128],
            sems.at[slot],
        )

    loads = [load(side * early + i, i) for i in range(early)]
    loads += [load(2 * early + i, early + i) for i in range(late)]
    load_new = pltpu.make_async_copy(new_ref, new_vmem, sems.at[early + late])
    send_shared = pltpu.make_async_copy(
        stage_ref.at[0:lat, 0:few], shared_ref, sems.at[early + late + 1]
    )
    send_direct = pltpu.make_async_copy(
        stage_ref.at[:, few : few + width], direct_ref, sems.at[early + late + 2]
    )
    for copy in loads[:early] + [load_new] + loads[early:]:
        copy.start()
    length = len_ref[0]
    high = length // 256
    r = lax.broadcasted_iota(jnp.int32, (16, 128), 0)
    c = lax.broadcasted_iota(jnp.int32, (16, 128), 1)
    note = jnp.where(
        (r == 0) & (c == 0), high, jnp.where((r == 0) & (c == 1), length - high * 256, 0)
    ).astype(jnp.float32)
    stage_ref[lat + 16 : lat + 32, few + 128 : few + 256] = note.astype(jnp.bfloat16)
    for copy in loads[:early]:
        copy.wait()
    send_shared.start()
    load_new.wait()
    stage_ref[lat : lat + 16, few : few + KVR] = new_vmem[:, 0:KVR]
    stage_ref[lat + 16 : lat + 32, few : few + lat - KVR] = new_vmem[:, KVR:lat]
    for copy in loads[early:]:
        copy.wait()
    send_direct.start()
    send_shared.wait()
    send_direct.wait()


def run_bias(width, first, core, valid):
    lane = lax.broadcasted_iota(jnp.int32, (1, width), 1)
    position = lane + lane // 128 * 128 + 2 * first + core * 128
    return jnp.where(position < valid, 0.0, masked_value)


def own_kernel(blocks, len_ref, *refs):
    query_refs, (keys_ref, acc_ref, stat_ref, rows_ref) = refs[:blocks], refs[blocks:]
    to_row = lax.broadcasted_iota(jnp.int32, (128, 128), 0)
    from_row = lax.broadcasted_iota(jnp.int32, (128, 128), 1)
    reorder = jnp.where(from_row == to_row % 16 * 8 + to_row // 16, 1.0, 0.0).astype(jnp.bfloat16)
    for i, ref in enumerate(query_refs):
        rows_ref[i * 128 : (i + 1) * 128, :] = dot_nn(reorder, ref[...]).astype(jnp.bfloat16)
    valid = len_ref[0]
    full = keys_ref.shape[1]
    widths = [full // 2, full * 3 // 4, full]

    def attend(width):
        scores = dot_nn(rows_ref[...], keys_ref[:, 0:width]) + key_bias(width, valid)
        high = jnp.max(scores, axis=1, keepdims=True)
        weights = jnp.exp2((scores - high) * exp_scale)
        total = jnp.sum(weights, axis=1, keepdims=True)
        acc_ref[...] = dot_nt(weights.astype(jnp.bfloat16), keys_ref[0:KVR, 0:width])
        stat_ref[...] = pack_stats(high, total)

    least = 0
    for width in widths:
        pl.when((valid > least) & (valid <= width))(functools.partial(attend, width))
        least = width


def attend_own(valid, blocks, keys):
    rows = sum(b.shape[0] for b in blocks)
    width = keys.shape[1]
    return pl.pallas_call(
        functools.partial(own_kernel, len(blocks)),
        in_specs=[SMEM] + [VMEM] * (len(blocks) + 1),
        out_specs=[VMEM, VMEM, VMEM],
        out_shape=[
            jax.ShapeDtypeStruct((rows, KVR), jnp.float32),
            jax.ShapeDtypeStruct((rows, 128), jnp.float32),
            jax.ShapeDtypeStruct((rows, keys.shape[0]), jnp.bfloat16),
        ],
        compiler_params=pltpu.CompilerParams(vmem_limit_bytes=12 * 2**20),
        cost_estimate=small_cost,
        name="attend_own",
    )(valid, *blocks, keys)


def partner_length(part_ref):
    lat = part_ref.shape[0] - EXTRA
    row = part_ref[lat + 16 : lat + 32, 128:256].astype(jnp.float32)
    r = lax.broadcasted_iota(jnp.int32, row.shape, 0)
    c = lax.broadcasted_iota(jnp.int32, row.shape, 1)
    high = jnp.sum(jnp.where((r == 0) & (c == 0), row, 0.0))
    low = jnp.sum(jnp.where((r == 0) & (c == 1), row, 0.0))
    return (high * 256.0 + low).astype(jnp.int32)


def fold(scores, values, acc, high, total):
    new_high = functools.reduce(
        jnp.maximum, [jnp.max(s, axis=1, keepdims=True) for s in scores], high
    )
    rescale = jnp.exp2((high - new_high) * exp_scale)
    acc = acc * rescale
    total = total * rescale
    for s, v in zip(scores, values):
        weights = jnp.exp2((s - new_high) * exp_scale)
        total = total + jnp.sum(weights, axis=1, keepdims=True)
        acc = acc + v(weights.astype(jnp.bfloat16))
    return acc, new_high, total


def final_kernel(counts, offset_ref, *refs):
    states, refs = refs[: 3 * len(counts)], refs[3 * len(counts) :]
    parts, (new_ref, up_ref, out_ref, latent_ref) = refs[:6], refs[6:]
    pieces = [(g, 128 * i) for g, count in enumerate(counts) for i in range(count)]
    mine_ref, direct_ref = parts[0], parts[2]
    lat = mine_ref.shape[0]
    head = lax.axis_index("head")
    core, side = lax.rem(head, 2), lax.rem(head // 2, 2)
    ctx = lax.axis_index("ctx")
    z, pair = lax.rem(ctx, NZ), ctx // NZ
    length = partner_length(direct_ref)
    firsts = [side * SHARED, (1 - side) * SHARED, 2 * SHARED]
    biases = [
        run_bias(parts[3 * i + j].shape[1], firsts[j], core if i == 0 else 1 - core, length)
        for i in range(2)
        for j in range(3)
    ]

    def values_of(ref):
        return lambda w: dot_nt(w, ref[0:KVR, :])

    partner_new = jnp.concatenate(
        [direct_ref[lat : lat + 16, 0:KVR], direct_ref[lat + 16 : lat + 32, 0 : lat - KVR]], axis=1
    )
    new_keys = jnp.concatenate([new_ref[...], partner_new], axis=0)
    lane = lax.broadcasted_iota(jnp.int32, (16, 32), 1)
    line = lax.broadcasted_iota(jnp.int32, (16, 32), 0)
    key_offsets = jnp.zeros((16, 32), jnp.int32)
    for k in range(32):
        place = ((pair if k < 16 else 1 - pair) * NZ + z) * 16 + k % 16
        key_offsets = jnp.where(lane == k, offset_ref[place], key_offsets)
    new_bias = []
    for block in range(NZ):
        token = (pair * NZ + lax.rem(z + OFFSETS[block], NZ)) * 16
        token_offsets = jnp.zeros((16, 32), jnp.int32)
        for t in range(16):
            token_offsets = jnp.where(line == t, offset_ref[token + t], token_offsets)
        new_bias.append(jnp.where(key_offsets <= token_offsets, 0.0, masked_value))
    wide = lax.broadcasted_iota(jnp.int32, (128, 128), 1)
    levels = jnp.zeros((128, 128), jnp.float32)
    for tile in range(NZ // 2):
        both = pieces[2 * tile : 2 * tile + 2]
        rows = jnp.concatenate([states[3 * g + 2][r : r + 128, :] for g, r in both], axis=0)
        stat = jnp.concatenate([states[3 * g + 1][r : r + 128, :] for g, r in both], axis=0)
        bias = jnp.concatenate([new_bias[2 * tile]] * 8 + [new_bias[2 * tile + 1]] * 8, axis=0)
        acc, high, total = fold(
            [dot_nn(rows, ref[0:lat, :]) + mask for ref, mask in zip(parts, biases)]
            + [dot_nt(rows, new_keys) + bias],
            [values_of(ref) for ref in parts] + [lambda w: dot_nn(w, new_keys[:, 0:KVR])],
            jnp.concatenate([states[3 * g][r : r + 128, :] for g, r in both], axis=0),
            stat[:, 0:1],
            stat[:, 1:2],
        )
        latent_ref[tile * 256 : (tile + 1) * 256, :] = (acc * (1.0 / total)).astype(jnp.bfloat16)
        level = high * exp_scale + jnp.log2(total)
        levels = jnp.where(wide == 2 * tile, level[:128], levels)
        levels = jnp.where(wide == 2 * tile + 1, level[128:], levels)
    slots = [lax.rem(z + OFFSETS[block], NZ) for block in range(NZ)]
    for head in range(8):
        latent = jnp.concatenate(
            [latent_ref[b * 128 + head * 16 : b * 128 + head * 16 + 16, :] for b in range(NZ)], axis=0
        )
        result = dot_nn(latent, up_ref[head]).astype(jnp.bfloat16)
        for block in range(NZ):
            out_ref[slots[block], head * 16 : head * 16 + 16, :] = result[block * 16 : block * 16 + 16]
    flat = levels.T
    p0 = flat.astype(jnp.bfloat16).astype(jnp.float32)
    p1 = (flat - p0).astype(jnp.bfloat16).astype(jnp.float32)
    p2 = flat - p0 - p1
    r = lax.broadcasted_iota(jnp.int32, (STAT, 128), 0)
    for block in range(NZ):
        stats = jnp.where(
            r == 0,
            p0[block : block + 1],
            jnp.where(r == 1, p1[block : block + 1], jnp.where(r == 2, p2[block : block + 1], 0.0)),
        )
        out_ref[slots[block], 128 : 128 + STAT, :] = stats.astype(jnp.bfloat16)


def merge_kernel(part_ref, out_ref, order_ref):
    levels = []
    for source in range(NZ):
        stats = part_ref[source, 128 : 128 + STAT, :].astype(jnp.float32)
        levels.append(stats[0:1] + stats[1:2] + stats[2:3])
    level = jnp.concatenate(levels, axis=0)
    factor = jnp.exp2(level - jnp.max(level, axis=0, keepdims=True))
    factor = factor / jnp.sum(factor, axis=0, keepdims=True)
    factor = jnp.concatenate([factor, jnp.zeros((128 - NZ, 128), jnp.float32)], axis=0).T
    total = jnp.zeros((128, VDIM), jnp.float32)
    for source in range(NZ):
        total = total + part_ref[source, 0:128, :].astype(jnp.float32) * factor[:, source : source + 1]
    for head in range(8):
        order_ref[pl.ds(head, 16, stride=8), :] = total[head * 16 : head * 16 + 16]
    out_ref[...] = order_ref[...].astype(jnp.bfloat16)


def shards(queries, cache, new_latents, cache_lengths, new_offsets, value_up_weight):
    own_tokens, head_local, lat = queries.shape
    rows = own_tokens * head_local
    z = lax.axis_index("ctx") % NZ
    keys = cache.T

    def across(a):
        moves = [
            (c * 16 + h, ((c + NZ) % 16) * 16 + (h + 8) % 16) for c in range(16) for h in range(16)
        ]
        return lax.ppermute(a, ("ctx", "head"), moves)

    def swap(a):
        return lax.ppermute(a, "head", [(h, h ^ 1) for h in range(16)])

    def shift(a, step):
        return lax.ppermute(
            a, "ctx", [(c, c // NZ * NZ + (c + step) % NZ) for c in range(16)]
        )

    own = queries.reshape(rows, lat)
    up1, down1 = shift(own, 1), shift(own, -1)

    width = cache.shape[0] // 2
    hbm = pl.BlockSpec(memory_space=pltpu.HBM)
    shared, direct = pl.pallas_call(
        pack_kernel,
        in_specs=[SMEM, hbm, hbm],
        out_specs=[hbm, hbm],
        out_shape=[
            jax.ShapeDtypeStruct((lat, SHARED), jnp.bfloat16),
            jax.ShapeDtypeStruct((lat + EXTRA, width - 2 * SHARED), jnp.bfloat16),
        ],
        scratch_shapes=[
            pltpu.VMEM((lat + EXTRA, width - SHARED), jnp.bfloat16),
            pltpu.VMEM((own_tokens, lat), jnp.bfloat16),
            pltpu.SemaphoreType.DMA(((width - SHARED) // 128 + 3,)),
        ],
        compiler_params=pltpu.CompilerParams(vmem_limit_bytes=4 * 2**20),
        name="pack",
    )(
        cache_lengths,
        pltpu.with_memory_space_constraint(keys, pltpu.HBM),
        pltpu.with_memory_space_constraint(new_latents, pltpu.HBM),
    )
    mine, direct = across(shared), across(direct)

    up1, down1 = lax.optimization_barrier((up1, down1))
    up2, down2 = shift(up1, 1), shift(down1, -1)
    state1 = attend_own(cache_lengths, [own, up1, down1], keys)
    other = lax.ppermute(mine, "head", [(h, h ^ 2) for h in range(16)])
    up2, down2, state1 = lax.optimization_barrier((up2, down2, state1))
    up3, down3 = shift(up2, 1), shift(down2, -1)
    four = lax.ppermute(
        jnp.where(z % 2 == 0, up2, down2),
        "ctx",
        [(c, c // NZ * NZ + (c + (2 if c % 2 == 0 else -2)) % NZ) for c in range(16)],
    )
    state2 = attend_own(cache_lengths, [up2, down2], keys)
    up3, down3, four, state2, mine, other, direct = lax.optimization_barrier(
        (up3, down3, four, state2, mine, other, direct)
    )
    far_mine, far_other, far_direct = swap(mine), swap(other), swap(direct)
    state3 = attend_own(cache_lengths, [up3, down3, four], keys)
    far_mine, far_other, far_direct, state3 = lax.optimization_barrier((far_mine, far_other, far_direct, state3))
    states = [part for state in (state1, state2, state3) for part in state]
    parts = pl.pallas_call(
        functools.partial(final_kernel, [3, 2, 3]),
        in_specs=[SMEM] + [VMEM] * 17,
        out_specs=VMEM,
        out_shape=jax.ShapeDtypeStruct((NZ, rows + STAT, VDIM), jnp.bfloat16),
        scratch_shapes=[pltpu.VMEM((NZ * rows, KVR), jnp.bfloat16)],
        compiler_params=pltpu.CompilerParams(vmem_limit_bytes=16 * 2**20),
        cost_estimate=small_cost,
        name="attend_final",
    )(new_offsets, *states, mine, other, direct, far_mine, far_other, far_direct, new_latents, value_up_weight)
    got = lax.all_to_all(
        parts, "ctx", 0, 0, axis_index_groups=[[*range(NZ)], [*range(NZ, 2 * NZ)]], tiled=True
    )
    out = pl.pallas_call(
        merge_kernel,
        in_specs=[VMEM],
        out_specs=VMEM,
        out_shape=jax.ShapeDtypeStruct((rows, VDIM), jnp.bfloat16),
        scratch_shapes=[pltpu.VMEM((rows, VDIM), jnp.float32)],
        name="merge",
    )(pltpu.with_memory_space_constraint(got, pltpu.VMEM))
    return out.reshape(own_tokens, head_local, VDIM)


def solution(mesh):
    return jax.shard_map(
        shards,
        mesh=mesh,
        in_specs=(
            P("ctx", "head", None),
            P("ctx", None),
            P("ctx", None),
            P("ctx"),
            P(),
            P("head", None, None),
        ),
        out_specs=P("ctx", "head", None),
        check_vma=False,
    )
```

```python
import functools

import jax
import jax.numpy as jnp
from jax import lax
from jax.experimental import pallas as pl
from jax.experimental.pallas import tpu as pltpu
from jax.sharding import PartitionSpec as P

KVR = 512
VDIM = 128
EXTRA = 32
STAT = 16
NZ = 8
OFFSETS = [0, 7, 1, 6, 2, 5, 3, 4]
SHARED = 256

exp_scale = 192.0 ** (-0.5) * 1.4426950408889634
masked_value = -1e30
NT = (((1,), (1,)), ((), ()))
small_cost = pl.CostEstimate(flops=10**6, bytes_accessed=10**4, transcendentals=0)
VMEM = pl.BlockSpec(memory_space=pltpu.VMEM)
SMEM = pl.BlockSpec(memory_space=pltpu.SMEM)


def dot_nt(a, b):
    return lax.dot_general(a, b, NT, preferred_element_type=jnp.float32)


def dot_nn(a, b):
    return jnp.dot(a, b, preferred_element_type=jnp.float32)


def pack_stats(high, total):
    lane = lax.broadcasted_iota(jnp.int32, (high.shape[0], 128), 1)
    return jnp.where(lane == 0, high, total)


def key_bias(width, valid):
    position = lax.broadcasted_iota(jnp.int32, (1, width), 1)
    return jnp.where(position < valid, 0.0, masked_value)


def runs_of(keys_ref, stage_ref, sems, first, count):
    core = lax.rem(lax.axis_index("head"), 2)
    copies = []
    for i in range(count):
        place = pl.multiple_of((2 * (first + i) + core) * 128, 128)
        copies.append(
            pltpu.make_async_copy(
                keys_ref.at[:, pl.ds(place, 128)],
                stage_ref.at[0 : keys_ref.shape[0], i * 128 : (i + 1) * 128],
                sems.at[i],
            )
        )
    return copies


def pack_shared_kernel(keys_ref, shared_ref, stage_ref, sems):
    side = lax.rem(lax.axis_index("head") // 2, 2)
    count = shared_ref.shape[1] // 128
    loads = runs_of(keys_ref, stage_ref, sems, side * count, count)
    send = pltpu.make_async_copy(stage_ref, shared_ref, sems.at[count])
    for copy in loads:
        copy.start()
    for copy in loads:
        copy.wait()
    send.start()
    send.wait()


def pack_direct_kernel(len_ref, keys_ref, new_ref, direct_ref, stage_ref, new_vmem, sems):
    lat, count = keys_ref.shape[0], direct_ref.shape[1] // 128
    loads = runs_of(keys_ref, stage_ref, sems, 2 * SHARED // 128, count)
    load_new = pltpu.make_async_copy(new_ref, new_vmem, sems.at[count])
    send = pltpu.make_async_copy(stage_ref, direct_ref, sems.at[count + 1])
    load_new.start()
    for copy in loads:
        copy.start()
    length = len_ref[0]
    high = length // 256
    r = lax.broadcasted_iota(jnp.int32, (16, 128), 0)
    c = lax.broadcasted_iota(jnp.int32, (16, 128), 1)
    note = jnp.where(
        (r == 0) & (c == 0), high, jnp.where((r == 0) & (c == 1), length - high * 256, 0)
    ).astype(jnp.float32)
    stage_ref[lat + 16 : lat + 32, 128:256] = note.astype(jnp.bfloat16)
    load_new.wait()
    stage_ref[lat : lat + 16, 0:KVR] = new_vmem[:, 0:KVR]
    stage_ref[lat + 16 : lat + 32, 0 : lat - KVR] = new_vmem[:, KVR:lat]
    for copy in loads:
        copy.wait()
    send.start()
    send.wait()


def run_bias(width, first, core, valid):
    lane = lax.broadcasted_iota(jnp.int32, (1, width), 1)
    position = lane + lane // 128 * 128 + 2 * first + core * 128
    return jnp.where(position < valid, 0.0, masked_value)


def own_kernel(blocks, len_ref, *refs):
    query_refs, (keys_ref, acc_ref, stat_ref, rows_ref) = refs[:blocks], refs[blocks:]
    to_row = lax.broadcasted_iota(jnp.int32, (128, 128), 0)
    from_row = lax.broadcasted_iota(jnp.int32, (128, 128), 1)
    reorder = jnp.where(from_row == to_row % 16 * 8 + to_row // 16, 1.0, 0.0).astype(jnp.bfloat16)
    for i, ref in enumerate(query_refs):
        rows_ref[i * 128 : (i + 1) * 128, :] = dot_nn(reorder, ref[...]).astype(jnp.bfloat16)
    valid = len_ref[0]
    full = keys_ref.shape[1]
    widths = [full // 2, full * 3 // 4, full]

    def attend(width):
        scores = dot_nn(rows_ref[...], keys_ref[:, 0:width]) + key_bias(width, valid)
        high = jnp.max(scores, axis=1, keepdims=True)
        weights = jnp.exp2((scores - high) * exp_scale)
        total = jnp.sum(weights, axis=1, keepdims=True)
        acc_ref[...] = dot_nt(weights.astype(jnp.bfloat16), keys_ref[0:KVR, 0:width])
        stat_ref[...] = pack_stats(high, total)

    least = 0
    for width in widths:
        pl.when((valid > least) & (valid <= width))(functools.partial(attend, width))
        least = width


def attend_own(valid, blocks, keys):
    rows = sum(b.shape[0] for b in blocks)
    width = keys.shape[1]
    return pl.pallas_call(
        functools.partial(own_kernel, len(blocks)),
        in_specs=[SMEM] + [VMEM] * (len(blocks) + 1),
        out_specs=[VMEM, VMEM, VMEM],
        out_shape=[
            jax.ShapeDtypeStruct((rows, KVR), jnp.float32),
            jax.ShapeDtypeStruct((rows, 128), jnp.float32),
            jax.ShapeDtypeStruct((rows, keys.shape[0]), jnp.bfloat16),
        ],
        compiler_params=pltpu.CompilerParams(vmem_limit_bytes=12 * 2**20),
        cost_estimate=small_cost,
        name="attend_own",
    )(valid, *blocks, keys)


def partner_length(part_ref):
    lat = part_ref.shape[0] - EXTRA
    row = part_ref[lat + 16 : lat + 32, 128:256].astype(jnp.float32)
    r = lax.broadcasted_iota(jnp.int32, row.shape, 0)
    c = lax.broadcasted_iota(jnp.int32, row.shape, 1)
    high = jnp.sum(jnp.where((r == 0) & (c == 0), row, 0.0))
    low = jnp.sum(jnp.where((r == 0) & (c == 1), row, 0.0))
    return (high * 256.0 + low).astype(jnp.int32)


def fold(scores, values, acc, high, total):
    new_high = functools.reduce(
        jnp.maximum, [jnp.max(s, axis=1, keepdims=True) for s in scores], high
    )
    rescale = jnp.exp2((high - new_high) * exp_scale)
    acc = acc * rescale
    total = total * rescale
    for s, v in zip(scores, values):
        weights = jnp.exp2((s - new_high) * exp_scale)
        total = total + jnp.sum(weights, axis=1, keepdims=True)
        acc = acc + v(weights.astype(jnp.bfloat16))
    return acc, new_high, total


def final_kernel(counts, offset_ref, *refs):
    states, refs = refs[: 3 * len(counts)], refs[3 * len(counts) :]
    parts, (new_ref, up_ref, out_ref, latent_ref) = refs[:6], refs[6:]
    pieces = [(g, 128 * i) for g, count in enumerate(counts) for i in range(count)]
    mine_ref, direct_ref = parts[0], parts[2]
    lat = mine_ref.shape[0]
    head = lax.axis_index("head")
    core, side = lax.rem(head, 2), lax.rem(head // 2, 2)
    ctx = lax.axis_index("ctx")
    z, pair = lax.rem(ctx, NZ), ctx // NZ
    length = partner_length(direct_ref)
    firsts = [side * SHARED, (1 - side) * SHARED, 2 * SHARED]
    biases = [
        run_bias(parts[3 * i + j].shape[1], firsts[j], core if i == 0 else 1 - core, length)
        for i in range(2)
        for j in range(3)
    ]

    def values_of(ref):
        return lambda w: dot_nt(w, ref[0:KVR, :])

    partner_new = jnp.concatenate(
        [direct_ref[lat : lat + 16, 0:KVR], direct_ref[lat + 16 : lat + 32, 0 : lat - KVR]], axis=1
    )
    new_keys = jnp.concatenate([new_ref[...], partner_new], axis=0)
    lane = lax.broadcasted_iota(jnp.int32, (16, 32), 1)
    line = lax.broadcasted_iota(jnp.int32, (16, 32), 0)
    key_offsets = jnp.zeros((16, 32), jnp.int32)
    for k in range(32):
        place = ((pair if k < 16 else 1 - pair) * NZ + z) * 16 + k % 16
        key_offsets = jnp.where(lane == k, offset_ref[place], key_offsets)
    new_bias = []
    for block in range(NZ):
        token = (pair * NZ + lax.rem(z + OFFSETS[block], NZ)) * 16
        token_offsets = jnp.zeros((16, 32), jnp.int32)
        for t in range(16):
            token_offsets = jnp.where(line == t, offset_ref[token + t], token_offsets)
        new_bias.append(jnp.where(key_offsets <= token_offsets, 0.0, masked_value))
    wide = lax.broadcasted_iota(jnp.int32, (128, 128), 1)
    levels = jnp.zeros((128, 128), jnp.float32)
    for tile in range(NZ // 2):
        both = pieces[2 * tile : 2 * tile + 2]
        rows = jnp.concatenate([states[3 * g + 2][r : r + 128, :] for g, r in both], axis=0)
        stat = jnp.concatenate([states[3 * g + 1][r : r + 128, :] for g, r in both], axis=0)
        bias = jnp.concatenate([new_bias[2 * tile]] * 8 + [new_bias[2 * tile + 1]] * 8, axis=0)
        acc, high, total = fold(
            [dot_nn(rows, ref[0:lat, :]) + mask for ref, mask in zip(parts, biases)]
            + [dot_nt(rows, new_keys) + bias],
            [values_of(ref) for ref in parts] + [lambda w: dot_nn(w, new_keys[:, 0:KVR])],
            jnp.concatenate([states[3 * g][r : r + 128, :] for g, r in both], axis=0),
            stat[:, 0:1],
            stat[:, 1:2],
        )
        latent_ref[tile * 256 : (tile + 1) * 256, :] = (acc * (1.0 / total)).astype(jnp.bfloat16)
        level = high * exp_scale + jnp.log2(total)
        levels = jnp.where(wide == 2 * tile, level[:128], levels)
        levels = jnp.where(wide == 2 * tile + 1, level[128:], levels)
    slots = [lax.rem(z + OFFSETS[block], NZ) for block in range(NZ)]
    for head in range(8):
        latent = jnp.concatenate(
            [latent_ref[b * 128 + head * 16 : b * 128 + head * 16 + 16, :] for b in range(NZ)], axis=0
        )
        result = dot_nn(latent, up_ref[head]).astype(jnp.bfloat16)
        for block in range(NZ):
            out_ref[slots[block], head * 16 : head * 16 + 16, :] = result[block * 16 : block * 16 + 16]
    flat = levels.T
    p0 = flat.astype(jnp.bfloat16).astype(jnp.float32)
    p1 = (flat - p0).astype(jnp.bfloat16).astype(jnp.float32)
    p2 = flat - p0 - p1
    r = lax.broadcasted_iota(jnp.int32, (STAT, 128), 0)
    for block in range(NZ):
        stats = jnp.where(
            r == 0,
            p0[block : block + 1],
            jnp.where(r == 1, p1[block : block + 1], jnp.where(r == 2, p2[block : block + 1], 0.0)),
        )
        out_ref[slots[block], 128 : 128 + STAT, :] = stats.astype(jnp.bfloat16)


def merge_kernel(part_ref, out_ref, order_ref):
    levels = []
    for source in range(NZ):
        stats = part_ref[source, 128 : 128 + STAT, :].astype(jnp.float32)
        levels.append(stats[0:1] + stats[1:2] + stats[2:3])
    level = jnp.concatenate(levels, axis=0)
    factor = jnp.exp2(level - jnp.max(level, axis=0, keepdims=True))
    factor = factor / jnp.sum(factor, axis=0, keepdims=True)
    factor = jnp.concatenate([factor, jnp.zeros((128 - NZ, 128), jnp.float32)], axis=0).T
    total = jnp.zeros((128, VDIM), jnp.float32)
    for source in range(NZ):
        total = total + part_ref[source, 0:128, :].astype(jnp.float32) * factor[:, source : source + 1]
    for head in range(8):
        order_ref[pl.ds(head, 16, stride=8), :] = total[head * 16 : head * 16 + 16]
    out_ref[...] = order_ref[...].astype(jnp.bfloat16)


def shards(queries, cache, new_latents, cache_lengths, new_offsets, value_up_weight):
    own_tokens, head_local, lat = queries.shape
    rows = own_tokens * head_local
    z = lax.axis_index("ctx") % NZ
    keys = cache.T

    def across(a):
        moves = [
            (c * 16 + h, ((c + NZ) % 16) * 16 + (h + 8) % 16) for c in range(16) for h in range(16)
        ]
        return lax.ppermute(a, ("ctx", "head"), moves)

    def swap(a):
        return lax.ppermute(a, "head", [(h, h ^ 1) for h in range(16)])

    def shift(a, step):
        return lax.ppermute(
            a, "ctx", [(c, c // NZ * NZ + (c + step) % NZ) for c in range(16)]
        )

    own = queries.reshape(rows, lat)
    up1, down1 = shift(own, 1), shift(own, -1)

    width = cache.shape[0] // 2
    hbm = pl.BlockSpec(memory_space=pltpu.HBM)
    keys_hbm = pltpu.with_memory_space_constraint(keys, pltpu.HBM)
    shared = pl.pallas_call(
        pack_shared_kernel,
        in_specs=[hbm],
        out_specs=hbm,
        out_shape=jax.ShapeDtypeStruct((lat, SHARED), jnp.bfloat16),
        scratch_shapes=[
            pltpu.VMEM((lat, SHARED), jnp.bfloat16),
            pltpu.SemaphoreType.DMA((SHARED // 128 + 1,)),
        ],
        compiler_params=pltpu.CompilerParams(vmem_limit_bytes=4 * 2**20),
        name="pack_shared",
    )(keys_hbm)
    rest = width - 2 * SHARED
    direct = pl.pallas_call(
        pack_direct_kernel,
        in_specs=[SMEM, hbm, hbm],
        out_specs=hbm,
        out_shape=jax.ShapeDtypeStruct((lat + EXTRA, rest), jnp.bfloat16),
        scratch_shapes=[
            pltpu.VMEM((lat + EXTRA, rest), jnp.bfloat16),
            pltpu.VMEM((own_tokens, lat), jnp.bfloat16),
            pltpu.SemaphoreType.DMA((rest // 128 + 2,)),
        ],
        compiler_params=pltpu.CompilerParams(vmem_limit_bytes=4 * 2**20),
        name="pack_direct",
    )(cache_lengths, keys_hbm, pltpu.with_memory_space_constraint(new_latents, pltpu.HBM))
    mine, direct = across(shared), across(direct)

    up1, down1 = lax.optimization_barrier((up1, down1))
    up2, down2 = shift(up1, 1), shift(down1, -1)
    state1 = attend_own(cache_lengths, [own, up1, down1], keys)
    other = lax.ppermute(mine, "head", [(h, h ^ 2) for h in range(16)])
    up2, down2, state1 = lax.optimization_barrier((up2, down2, state1))
    up3, down3 = shift(up2, 1), shift(down2, -1)
    four = lax.ppermute(
        jnp.where(z % 2 == 0, up2, down2),
        "ctx",
        [(c, c // NZ * NZ + (c + (2 if c % 2 == 0 else -2)) % NZ) for c in range(16)],
    )
    state2 = attend_own(cache_lengths, [up2, down2], keys)
    up3, down3, four, state2, mine, other, direct = lax.optimization_barrier(
        (up3, down3, four, state2, mine, other, direct)
    )
    far_mine, far_other, far_direct = swap(mine), swap(other), swap(direct)
    state3 = attend_own(cache_lengths, [up3, down3, four], keys)
    far_mine, far_other, far_direct, state3 = lax.optimization_barrier((far_mine, far_other, far_direct, state3))
    states = [part for state in (state1, state2, state3) for part in state]
    parts = pl.pallas_call(
        functools.partial(final_kernel, [3, 2, 3]),
        in_specs=[SMEM] + [VMEM] * 17,
        out_specs=VMEM,
        out_shape=jax.ShapeDtypeStruct((NZ, rows + STAT, VDIM), jnp.bfloat16),
        scratch_shapes=[pltpu.VMEM((NZ * rows, KVR), jnp.bfloat16)],
        compiler_params=pltpu.CompilerParams(vmem_limit_bytes=16 * 2**20),
        cost_estimate=small_cost,
        name="attend_final",
    )(new_offsets, *states, mine, other, direct, far_mine, far_other, far_direct, new_latents, value_up_weight)
    got = lax.all_to_all(
        parts, "ctx", 0, 0, axis_index_groups=[[*range(NZ)], [*range(NZ, 2 * NZ)]], tiled=True
    )
    out = pl.pallas_call(
        merge_kernel,
        in_specs=[VMEM],
        out_specs=VMEM,
        out_shape=jax.ShapeDtypeStruct((rows, VDIM), jnp.bfloat16),
        scratch_shapes=[pltpu.VMEM((rows, VDIM), jnp.float32)],
        name="merge",
    )(pltpu.with_memory_space_constraint(got, pltpu.VMEM))
    return out.reshape(own_tokens, head_local, VDIM)


def solution(mesh):
    return jax.shard_map(
        shards,
        mesh=mesh,
        in_specs=(
            P("ctx", "head", None),
            P("ctx", None),
            P("ctx", None),
            P("ctx"),
            P(),
            P("head", None, None),
        ),
        out_specs=P("ctx", "head", None),
        check_vma=False,
    )
```

```python
import functools

import jax
import jax.numpy as jnp
from jax import lax
from jax.experimental import pallas as pl
from jax.experimental.pallas import tpu as pltpu
from jax.sharding import PartitionSpec as P

KVR = 512
VDIM = 128
EXTRA = 32
STAT = 16
NZ = 8
OFFSETS = [7, 1, 6, 2, 0, 5, 3, 4]
SHARED = 256

exp_scale = 192.0 ** (-0.5) * 1.4426950408889634
masked_value = -1e30
NT = (((1,), (1,)), ((), ()))
small_cost = pl.CostEstimate(flops=10**6, bytes_accessed=10**4, transcendentals=0)
VMEM = pl.BlockSpec(memory_space=pltpu.VMEM)
SMEM = pl.BlockSpec(memory_space=pltpu.SMEM)


def dot_nt(a, b):
    return lax.dot_general(a, b, NT, preferred_element_type=jnp.float32)


def dot_nn(a, b):
    return jnp.dot(a, b, preferred_element_type=jnp.float32)


def pack_stats(high, total):
    lane = lax.broadcasted_iota(jnp.int32, (high.shape[0], 128), 1)
    return jnp.where(lane == 0, high, total)


def key_bias(width, valid):
    position = lax.broadcasted_iota(jnp.int32, (1, width), 1)
    return jnp.where(position < valid, 0.0, masked_value)


def pack_kernel(len_ref, keys_ref, new_ref, shared_ref, direct_ref, stage_ref, new_vmem, sems):
    head = lax.axis_index("head")
    core, side = lax.rem(head, 2), lax.rem(head // 2, 2)
    lat, few = shared_ref.shape
    width = direct_ref.shape[1]
    early, late = few // 128, width // 128

    def load(run, slot):
        place = pl.multiple_of((2 * run + core) * 128, 128)
        return pltpu.make_async_copy(
            keys_ref.at[:, pl.ds(place, 128)],
            stage_ref.at[0:lat, slot * 128 : (slot + 1) * 128],
            sems.at[slot],
        )

    loads = [load(side * early + i, i) for i in range(early)]
    loads += [load(2 * early + i, early + i) for i in range(late)]
    load_new = pltpu.make_async_copy(new_ref, new_vmem, sems.at[early + late])
    send_shared = pltpu.make_async_copy(
        stage_ref.at[0:lat, 0:few], shared_ref, sems.at[early + late + 1]
    )
    send_direct = pltpu.make_async_copy(
        stage_ref.at[:, few : few + width], direct_ref, sems.at[early + late + 2]
    )
    for copy in loads[:early] + [load_new] + loads[early:]:
        copy.start()
    length = len_ref[0]
    high = length // 256
    r = lax.broadcasted_iota(jnp.int32, (16, 128), 0)
    c = lax.broadcasted_iota(jnp.int32, (16, 128), 1)
    note = jnp.where(
        (r == 0) & (c == 0), high, jnp.where((r == 0) & (c == 1), length - high * 256, 0)
    ).astype(jnp.float32)
    stage_ref[lat + 16 : lat + 32, few + 128 : few + 256] = note.astype(jnp.bfloat16)
    for copy in loads[:early]:
        copy.wait()
    send_shared.start()
    load_new.wait()
    stage_ref[lat : lat + 16, few : few + KVR] = new_vmem[:, 0:KVR]
    stage_ref[lat + 16 : lat + 32, few : few + lat - KVR] = new_vmem[:, KVR:lat]
    for copy in loads[early:]:
        copy.wait()
    send_direct.start()
    send_shared.wait()
    send_direct.wait()


def run_bias(width, first, core, valid):
    lane = lax.broadcasted_iota(jnp.int32, (1, width), 1)
    position = lane + lane // 128 * 128 + 2 * first + core * 128
    return jnp.where(position < valid, 0.0, masked_value)


def own_kernel(blocks, len_ref, *refs):
    query_refs, (keys_ref, acc_ref, stat_ref, rows_ref) = refs[:blocks], refs[blocks:]
    to_row = lax.broadcasted_iota(jnp.int32, (128, 128), 0)
    from_row = lax.broadcasted_iota(jnp.int32, (128, 128), 1)
    reorder = jnp.where(from_row == to_row % 16 * 8 + to_row // 16, 1.0, 0.0).astype(jnp.bfloat16)
    for i, ref in enumerate(query_refs):
        rows_ref[i * 128 : (i + 1) * 128, :] = dot_nn(reorder, ref[...]).astype(jnp.bfloat16)
    valid = len_ref[0]
    full = keys_ref.shape[1]
    widths = [full // 2, full * 3 // 4, full]

    def attend(width):
        scores = dot_nn(rows_ref[...], keys_ref[:, 0:width]) + key_bias(width, valid)
        high = jnp.max(scores, axis=1, keepdims=True)
        weights = jnp.exp2((scores - high) * exp_scale)
        total = jnp.sum(weights, axis=1, keepdims=True)
        acc_ref[...] = dot_nt(weights.astype(jnp.bfloat16), keys_ref[0:KVR, 0:width])
        stat_ref[...] = pack_stats(high, total)

    least = 0
    for width in widths:
        pl.when((valid > least) & (valid <= width))(functools.partial(attend, width))
        least = width


def attend_own(valid, blocks, keys):
    rows = sum(b.shape[0] for b in blocks)
    width = keys.shape[1]
    return pl.pallas_call(
        functools.partial(own_kernel, len(blocks)),
        in_specs=[SMEM] + [VMEM] * (len(blocks) + 1),
        out_specs=[VMEM, VMEM, VMEM],
        out_shape=[
            jax.ShapeDtypeStruct((rows, KVR), jnp.float32),
            jax.ShapeDtypeStruct((rows, 128), jnp.float32),
            jax.ShapeDtypeStruct((rows, keys.shape[0]), jnp.bfloat16),
        ],
        compiler_params=pltpu.CompilerParams(vmem_limit_bytes=12 * 2**20),
        cost_estimate=small_cost,
        name="attend_own",
    )(valid, *blocks, keys)


def partner_length(part_ref):
    lat = part_ref.shape[0] - EXTRA
    row = part_ref[lat + 16 : lat + 32, 128:256].astype(jnp.float32)
    r = lax.broadcasted_iota(jnp.int32, row.shape, 0)
    c = lax.broadcasted_iota(jnp.int32, row.shape, 1)
    high = jnp.sum(jnp.where((r == 0) & (c == 0), row, 0.0))
    low = jnp.sum(jnp.where((r == 0) & (c == 1), row, 0.0))
    return (high * 256.0 + low).astype(jnp.int32)


def fold(scores, values, acc, high, total):
    new_high = functools.reduce(
        jnp.maximum, [jnp.max(s, axis=1, keepdims=True) for s in scores], high
    )
    rescale = jnp.exp2((high - new_high) * exp_scale)
    acc = acc * rescale
    total = total * rescale
    for s, v in zip(scores, values):
        weights = jnp.exp2((s - new_high) * exp_scale)
        total = total + jnp.sum(weights, axis=1, keepdims=True)
        acc = acc + v(weights.astype(jnp.bfloat16))
    return acc, new_high, total


def final_kernel(counts, offset_ref, *refs):
    states, refs = refs[: 3 * len(counts)], refs[3 * len(counts) :]
    parts, (new_ref, up_ref, out_ref, latent_ref) = refs[:6], refs[6:]
    pieces = [(g, 128 * i) for g, count in enumerate(counts) for i in range(count)]
    mine_ref, direct_ref = parts[0], parts[2]
    lat = mine_ref.shape[0]
    head = lax.axis_index("head")
    core, side = lax.rem(head, 2), lax.rem(head // 2, 2)
    ctx = lax.axis_index("ctx")
    z, pair = lax.rem(ctx, NZ), ctx // NZ
    length = partner_length(direct_ref)
    firsts = [side * SHARED, (1 - side) * SHARED, 2 * SHARED]
    biases = [
        run_bias(parts[3 * i + j].shape[1], firsts[j], core if i == 0 else 1 - core, length)
        for i in range(2)
        for j in range(3)
    ]

    def values_of(ref):
        return lambda w: dot_nt(w, ref[0:KVR, :])

    partner_new = jnp.concatenate(
        [direct_ref[lat : lat + 16, 0:KVR], direct_ref[lat + 16 : lat + 32, 0 : lat - KVR]], axis=1
    )
    new_keys = jnp.concatenate([new_ref[...], partner_new], axis=0)
    lane = lax.broadcasted_iota(jnp.int32, (16, 32), 1)
    line = lax.broadcasted_iota(jnp.int32, (16, 32), 0)
    key_offsets = jnp.zeros((16, 32), jnp.int32)
    for k in range(32):
        place = ((pair if k < 16 else 1 - pair) * NZ + z) * 16 + k % 16
        key_offsets = jnp.where(lane == k, offset_ref[place], key_offsets)
    new_bias = []
    for block in range(NZ):
        token = (pair * NZ + lax.rem(z + OFFSETS[block], NZ)) * 16
        token_offsets = jnp.zeros((16, 32), jnp.int32)
        for t in range(16):
            token_offsets = jnp.where(line == t, offset_ref[token + t], token_offsets)
        new_bias.append(jnp.where(key_offsets <= token_offsets, 0.0, masked_value))
    wide = lax.broadcasted_iota(jnp.int32, (128, 128), 1)
    levels = jnp.zeros((128, 128), jnp.float32)
    for tile in range(NZ // 2):
        both = pieces[2 * tile : 2 * tile + 2]
        rows = jnp.concatenate([states[3 * g + 2][r : r + 128, :] for g, r in both], axis=0)
        stat = jnp.concatenate([states[3 * g + 1][r : r + 128, :] for g, r in both], axis=0)
        bias = jnp.concatenate([new_bias[2 * tile]] * 8 + [new_bias[2 * tile + 1]] * 8, axis=0)
        acc, high, total = fold(
            [dot_nn(rows, ref[0:lat, :]) + mask for ref, mask in zip(parts, biases)]
            + [dot_nt(rows, new_keys) + bias],
            [values_of(ref) for ref in parts] + [lambda w: dot_nn(w, new_keys[:, 0:KVR])],
            jnp.concatenate([states[3 * g][r : r + 128, :] for g, r in both], axis=0),
            stat[:, 0:1],
            stat[:, 1:2],
        )
        latent_ref[tile * 256 : (tile + 1) * 256, :] = (acc * (1.0 / total)).astype(jnp.bfloat16)
        level = high * exp_scale + jnp.log2(total)
        levels = jnp.where(wide == 2 * tile, level[:128], levels)
        levels = jnp.where(wide == 2 * tile + 1, level[128:], levels)
    slots = [lax.rem(z + OFFSETS[block], NZ) for block in range(NZ)]
    for head in range(8):
        latent = jnp.concatenate(
            [latent_ref[b * 128 + head * 16 : b * 128 + head * 16 + 16, :] for b in range(NZ)], axis=0
        )
        result = dot_nn(latent, up_ref[head]).astype(jnp.bfloat16)
        for block in range(NZ):
            out_ref[slots[block], head * 16 : head * 16 + 16, :] = result[block * 16 : block * 16 + 16]
    flat = levels.T
    p0 = flat.astype(jnp.bfloat16).astype(jnp.float32)
    p1 = (flat - p0).astype(jnp.bfloat16).astype(jnp.float32)
    p2 = flat - p0 - p1
    r = lax.broadcasted_iota(jnp.int32, (STAT, 128), 0)
    for block in range(NZ):
        stats = jnp.where(
            r == 0,
            p0[block : block + 1],
            jnp.where(r == 1, p1[block : block + 1], jnp.where(r == 2, p2[block : block + 1], 0.0)),
        )
        out_ref[slots[block], 128 : 128 + STAT, :] = stats.astype(jnp.bfloat16)


def merge_kernel(part_ref, out_ref, order_ref):
    levels = []
    for source in range(NZ):
        stats = part_ref[source, 128 : 128 + STAT, :].astype(jnp.float32)
        levels.append(stats[0:1] + stats[1:2] + stats[2:3])
    level = jnp.concatenate(levels, axis=0)
    factor = jnp.exp2(level - jnp.max(level, axis=0, keepdims=True))
    factor = factor / jnp.sum(factor, axis=0, keepdims=True)
    factor = jnp.concatenate([factor, jnp.zeros((128 - NZ, 128), jnp.float32)], axis=0).T
    total = jnp.zeros((128, VDIM), jnp.float32)
    for source in range(NZ):
        total = total + part_ref[source, 0:128, :].astype(jnp.float32) * factor[:, source : source + 1]
    for head in range(8):
        order_ref[pl.ds(head, 16, stride=8), :] = total[head * 16 : head * 16 + 16]
    out_ref[...] = order_ref[...].astype(jnp.bfloat16)


def shards(queries, cache, new_latents, cache_lengths, new_offsets, value_up_weight):
    own_tokens, head_local, lat = queries.shape
    rows = own_tokens * head_local
    z = lax.axis_index("ctx") % NZ
    keys = cache.T

    def across(a):
        moves = [
            (c * 16 + h, ((c + NZ) % 16) * 16 + (h + 8) % 16) for c in range(16) for h in range(16)
        ]
        return lax.ppermute(a, ("ctx", "head"), moves)

    def swap(a):
        return lax.ppermute(a, "head", [(h, h ^ 1) for h in range(16)])

    def shift(a, step):
        return lax.ppermute(
            a, "ctx", [(c, c // NZ * NZ + (c + step) % NZ) for c in range(16)]
        )

    own = queries.reshape(rows, lat)
    up1, down1 = shift(own, 1), shift(own, -1)

    width = cache.shape[0] // 2
    hbm = pl.BlockSpec(memory_space=pltpu.HBM)
    shared, direct = pl.pallas_call(
        pack_kernel,
        in_specs=[SMEM, hbm, hbm],
        out_specs=[hbm, hbm],
        out_shape=[
            jax.ShapeDtypeStruct((lat, SHARED), jnp.bfloat16),
            jax.ShapeDtypeStruct((lat + EXTRA, width - 2 * SHARED), jnp.bfloat16),
        ],
        scratch_shapes=[
            pltpu.VMEM((lat + EXTRA, width - SHARED), jnp.bfloat16),
            pltpu.VMEM((own_tokens, lat), jnp.bfloat16),
            pltpu.SemaphoreType.DMA(((width - SHARED) // 128 + 3,)),
        ],
        compiler_params=pltpu.CompilerParams(vmem_limit_bytes=4 * 2**20),
        name="pack",
    )(
        cache_lengths,
        pltpu.with_memory_space_constraint(keys, pltpu.HBM),
        pltpu.with_memory_space_constraint(new_latents, pltpu.HBM),
    )
    mine, direct = across(shared), across(direct)

    up1, down1 = lax.optimization_barrier((up1, down1))
    up2, down2 = shift(up1, 1), shift(down1, -1)
    state1 = attend_own(cache_lengths, [up1, down1], keys)
    other = lax.ppermute(mine, "head", [(h, h ^ 2) for h in range(16)])
    up2, down2, state1 = lax.optimization_barrier((up2, down2, state1))
    up3, down3 = shift(up2, 1), shift(down2, -1)
    four = lax.ppermute(
        jnp.where(z % 2 == 0, up2, down2),
        "ctx",
        [(c, c // NZ * NZ + (c + (2 if c % 2 == 0 else -2)) % NZ) for c in range(16)],
    )
    state2 = attend_own(cache_lengths, [up2, down2, own], keys)
    up3, down3, four, state2, mine, other, direct = lax.optimization_barrier(
        (up3, down3, four, state2, mine, other, direct)
    )
    far_mine, far_other, far_direct = swap(mine), swap(other), swap(direct)
    state3 = attend_own(cache_lengths, [up3, down3, four], keys)
    far_mine, far_other, far_direct, state3 = lax.optimization_barrier((far_mine, far_other, far_direct, state3))
    states = [part for state in (state1, state2, state3) for part in state]
    parts = pl.pallas_call(
        functools.partial(final_kernel, [2, 3, 3]),
        in_specs=[SMEM] + [VMEM] * 17,
        out_specs=VMEM,
        out_shape=jax.ShapeDtypeStruct((NZ, rows + STAT, VDIM), jnp.bfloat16),
        scratch_shapes=[pltpu.VMEM((NZ * rows, KVR), jnp.bfloat16)],
        compiler_params=pltpu.CompilerParams(vmem_limit_bytes=16 * 2**20),
        cost_estimate=small_cost,
        name="attend_final",
    )(new_offsets, *states, mine, other, direct, far_mine, far_other, far_direct, new_latents, value_up_weight)
    got = lax.all_to_all(
        parts, "ctx", 0, 0, axis_index_groups=[[*range(NZ)], [*range(NZ, 2 * NZ)]], tiled=True
    )
    out = pl.pallas_call(
        merge_kernel,
        in_specs=[VMEM],
        out_specs=VMEM,
        out_shape=jax.ShapeDtypeStruct((rows, VDIM), jnp.bfloat16),
        scratch_shapes=[pltpu.VMEM((rows, VDIM), jnp.float32)],
        name="merge",
    )(pltpu.with_memory_space_constraint(got, pltpu.VMEM))
    return out.reshape(own_tokens, head_local, VDIM)


def solution(mesh):
    return jax.shard_map(
        shards,
        mesh=mesh,
        in_specs=(
            P("ctx", "head", None),
            P("ctx", None),
            P("ctx", None),
            P("ctx"),
            P(),
            P("head", None, None),
        ),
        out_specs=P("ctx", "head", None),
        check_vma=False,
    )
```
